32 devices in a mesh: grp: 8 (over y, x, core), blk: 4 (over z).
Axes of the slice: x: 2, y: 2, z: 4, core: 2. Of those that a mesh axis runs over, the one named last changes fastest.
Arguments:
- tiles_near: bfloat16 [1024, 256, 256], P(('grp', 'blk')), may hold values from -0.09375 to 0.09375
- near_cols: int32 [32, 32], P(('grp', 'blk')), may hold values from 0 to 3
- tiles_far: bfloat16 [768, 256, 256], P(('grp', 'blk')), may hold values from -0.09375 to 0.09375
- far_groups: int32 [32, 24], P(('grp', 'blk')), may hold values from 0 to 7, as said below
- need_blocks: int32 [32, 8], P(('grp', 'blk')), may hold values from -1 to 3, as said below
- start_vectors: bfloat16 [32768, 128], P(('grp', 'blk')), may hold values from -6 to 6
Outputs:
- vectors: float32 [32768, 128], P(('grp', 'blk'))
The draws below stay inside these ranges and needn't reach their ends.
Inputs may be any that keep to these rules, and one draw needn't show every extreme that they name: need_blocks[d, h] is -1 for d's own group and for groups d reads nothing from, else a row block index below 4 of the device of group h at d's position along blk; every device reads from at least one other group. far_groups[d, t] is a group h with need_blocks[d, h] >= 0.
All inputs are finite; a program needn't handle non-finite values.
Results may differ from the reference program's by a relative error of at most 0.0029.
Values may be sent and summed in bfloat16 or wider, within the bound.
No kernel may reach another device: no remote copies, remote signals or barrier semaphores. Data moves between devices by JAX's collectives and lax.ppermute only.
A program may use at most 128 MiB of HBM per device.

```python
import jax
import jax.numpy as jnp
from jax import lax

K = 128
TILE = 256
RB_DEV = 4
NPS = 2
FAR_RB = 6
ITERS = 2
NB = 128
ROWS = 32768
TN = 32
TF = 24
N_GRP = 8
N_BLK = 4
DEVICES = 32


def linked_draw(key):
    folded = jax.random.fold_in(key, 11)
    key_named, key_block, key_picked = jax.random.split(folded, 3)
    device = jnp.arange(DEVICES, dtype=jnp.int32)
    group_id = device // N_BLK
    groups = jnp.arange(N_GRP, dtype=jnp.int32)
    named = jax.random.randint(key_named, (DEVICES, N_GRP), 0, 10) < 6
    named = named & (groups[None, :] != group_id[:, None])
    named = named | (groups[None, :] == ((group_id + 1) % N_GRP)[:, None])
    needed = jnp.where(named, jax.random.randint(key_block, (DEVICES, N_GRP), 0, RB_DEV), -1).astype(jnp.int32)
    ranked = jnp.argsort(jnp.where(named, 0, 1).astype(jnp.int32) * N_GRP + groups[None, :], axis=1, stable=True).astype(jnp.int32)
    counted = jnp.sum(named.astype(jnp.int32), axis=1)
    picked = jax.random.randint(key_picked, (DEVICES, TF), 0, 1 << 20) % counted[:, None]
    far_list = jnp.take_along_axis(ranked, picked, axis=1).astype(jnp.int32)
    return (needed, far_list)


def draw_need_blocks(key, part):
    needed, far_list = linked_draw(key)
    return needed


def draw_far_groups(key, part):
    needed, far_list = linked_draw(key)
    return far_list


def set_ends(array, rng, smallest, largest):
    longest = array.shape.index(max(array.shape))
    spots = []
    for shift in (0, 1):
        where = [jax.random.randint(jax.random.fold_in(rng, axis), (), 0, length) for axis, length in enumerate(array.shape)]
        where[longest] = (where[longest] + shift) % array.shape[longest]
        spots.append(tuple(where))
    return array.at[spots[0]].set(smallest).at[spots[1]].set(largest)


def levels(rng, shape, pieces, least, largest):
    loudness = 1.0
    for dim, blocks in pieces:
        draws = jax.random.uniform(jax.random.fold_in(jax.random.fold_in(rng, 6), dim), (blocks,), jnp.float32, least / len(pieces), largest / len(pieces))
        loudness = loudness * jnp.repeat(jnp.exp(draws), shape[dim] // blocks).reshape((-1,) + (1,) * (len(shape) - 1 - dim))
    return loudness


def scatter_about(key, dims, scale, reach, pieces=(), kind=jnp.bfloat16):
    entries = scale * jax.random.normal(key, dims, jnp.float32)
    if pieces:
        entries = entries * levels(key, dims, pieces, -0.22, 0.18)
    return jnp.clip(entries, -reach, reach).astype(kind)


def setup_inputs(seed: int = 0) -> dict:
    key_list = jax.random.split(jax.random.key(seed), 7)
    tiles_near = scatter_about(key_list[0], (DEVICES * TN, TILE, TILE), (TILE * (N_BLK * NPS + FAR_RB)) ** -0.5, 0.09375, ((0, 32),))
    near_cols = set_ends(jax.random.randint(key_list[1], (DEVICES, TN), 0, RB_DEV), jax.random.fold_in(key_list[1], 1), 0, RB_DEV - 1).astype(jnp.int32)
    tiles_far = scatter_about(key_list[2], (DEVICES * TF, TILE, TILE), (TILE * (N_BLK * NPS + FAR_RB)) ** -0.5, 0.09375, ((0, 32),))
    far_groups = draw_far_groups(jax.random.fold_in(key_list[6], 71), 0)
    need_blocks = draw_need_blocks(jax.random.fold_in(key_list[6], 71), 0)
    start_vectors = scatter_about(key_list[5], (ROWS, K), 1.0, 6.0, ((0, 32),))
    return {"tiles_near": tiles_near, "near_cols": near_cols, "tiles_far": tiles_far, "far_groups": far_groups, "need_blocks": need_blocks, "start_vectors": start_vectors}


def reference(tiles_near, near_cols, tiles_far, far_groups, need_blocks, start_vectors):
    device_ids = jnp.arange(DEVICES, dtype=jnp.int32)
    near_all = tiles_near.reshape(DEVICES, RB_DEV, N_BLK * NPS, TILE, TILE)
    near_index = near_cols.reshape(DEVICES, RB_DEV, N_BLK * NPS)
    far_all = tiles_far.reshape(DEVICES, RB_DEV, FAR_RB, TILE, TILE)
    far_index = far_groups.reshape(DEVICES, RB_DEV, FAR_RB)
    source_pos = (jnp.arange(N_BLK * NPS, dtype=jnp.int32) // NPS).astype(jnp.int32)
    current = start_vectors
    vectors = start_vectors.astype(jnp.float32)
    for iteration in range(ITERS):
        block_table = current.reshape(NB, TILE, K)

        def one_device(inputs):
            device, near_tiles, near_ids, far_tiles, far_ids, needed = inputs
            group_id = device // N_BLK
            position = device % N_BLK
            near_block = ((group_id * N_BLK + source_pos)[None, :] * RB_DEV + near_ids).astype(jnp.int32)
            near_rows = block_table[near_block].astype(jnp.float32)
            near_part = jnp.einsum('rnij,rnjk->rik', near_tiles.astype(jnp.float32), near_rows)
            far_block = ((far_ids * N_BLK + position) * RB_DEV + needed[far_ids]).astype(jnp.int32)
            far_rows = block_table[far_block].astype(jnp.float32)
            far_part = jnp.einsum('rnij,rnjk->rik', far_tiles.astype(jnp.float32), far_rows)
            return near_part + far_part
        product = lax.map(one_device, (device_ids, near_all, near_index, far_all, far_index, need_blocks))
        flat_rows = product.reshape(ROWS, K)
        gram = jnp.dot(flat_rows.T.astype(jnp.float32), flat_rows.astype(jnp.float32), precision=lax.Precision.HIGHEST, preferred_element_type=jnp.float32) / ROWS
        factor = jnp.linalg.cholesky(gram)
        identity_matrix = jnp.eye(K, dtype=jnp.float32)
        inverse = lax.linalg.triangular_solve(factor, identity_matrix, left_side=True, lower=True).T
        vectors = jnp.dot(flat_rows.astype(jnp.float32), inverse.astype(jnp.float32), precision=lax.Precision.HIGHEST, preferred_element_type=jnp.float32)
        current = vectors.astype(jnp.bfloat16)
    return vectors
```

```python
import functools

import jax
import jax.numpy as jnp
from jax import lax
from jax.experimental import pallas as pl
from jax.experimental.pallas import tpu as pltpu
from jax.sharding import PartitionSpec as P

ITERS = 2
AXES = ("grp", "blk")
HIGHEST = lax.Precision.HIGHEST
INFLATION_MAX = 1.05
CORRECTION_MAX = 4e-6
VMEM = pl.BlockSpec(memory_space=pltpu.VMEM)
SMEM = pl.BlockSpec(memory_space=pltpu.SMEM)
F32 = jnp.float32
BF16 = jnp.bfloat16


def mm(a, b):
    return jnp.dot(a, b, precision=HIGHEST, preferred_element_type=F32)


def mm_nt(a, b):
    return lax.dot_general(a, b, (((1,), (1,)), ((), ())), precision=HIGHEST, preferred_element_type=F32)


def mm_tn(a, b):
    return lax.dot_general(a, b, (((0,), (0,)), ((), ())), precision=HIGHEST, preferred_element_type=F32)


def cost(flops, nbytes):
    return pl.CostEstimate(flops=flops, bytes_accessed=nbytes, transcendentals=0)


def inverse_factor(gram, work):
    n = gram.shape[0]
    rows = lax.broadcasted_iota(jnp.int32, (n, n), 0)
    cols = lax.broadcasted_iota(jnp.int32, (n, n), 1)
    on_diag = rows == cols
    eye = on_diag.astype(F32)
    weight = jnp.where(rows > cols, 1.0, jnp.where(on_diag, 0.5, 0.0)).astype(F32)
    on_diag_values = jnp.where(on_diag, gram, 0.0)
    scale_row = lax.rsqrt(jnp.sum(on_diag_values, axis=0, keepdims=True))
    scale_col = lax.rsqrt(jnp.sum(on_diag_values, axis=1, keepdims=True))
    base = gram * scale_col * scale_row - eye
    low = weight * base
    size = jnp.float32(0)
    for _ in range(2):
        moved = mm(low, base)
        crossed = mm_nt(low + moved - base, low)
        error = base - low - moved + crossed - low * eye
        step = weight * error
        size = jnp.sum(step * step)
        low = low + step - mm(step, low)
    work[0] = eye - low

    @pl.when(jnp.logical_not(size <= CORRECTION_MAX))
    def _():
        work[0] = eye
        work[1] = base + eye

        def eliminate(j, carry):
            left = work[1]
            pivot_row = work[1, pl.ds(j, 1), :]
            pivot = jnp.sum(jnp.where(cols[:1] == j, pivot_row, 0.0), axis=1, keepdims=True)
            column = jnp.sum(jnp.where(cols == j, left, 0.0), axis=1, keepdims=True)
            factor = jnp.where(rows[:, :1] > j, column / pivot, 0.0)
            right_row = work[0, pl.ds(j, 1), :]
            work[1] = left - factor * pivot_row
            work[0] = work[0] - factor * right_row
            work[0, pl.ds(j, 1), :] = right_row * lax.rsqrt(pivot)
            return carry

        lax.fori_loop(0, n, eliminate, 0)

    inverse = work[0]
    inflation = jnp.sum(inverse * inverse) / n
    return inverse * scale_row, inflation


def factor_kernel(total_rows, gram_ref, inverse_ref, fine_ref, work):
    inverse, inflation = inverse_factor(gram_ref[...] / total_rows, work)
    inverse_ref[...] = inverse
    fine_ref[0] = (inflation <= INFLATION_MAX).astype(jnp.int32)


def factor(gram, total_rows):
    n = gram.shape[0]
    return pl.pallas_call(
        functools.partial(factor_kernel, total_rows),
        out_shape=(jax.ShapeDtypeStruct((n, n), F32), jax.ShapeDtypeStruct((1,), jnp.int32)),
        in_specs=[VMEM],
        out_specs=(VMEM, SMEM),
        scratch_shapes=[pltpu.VMEM((2, n, n), F32)],
        cost_estimate=cost(2 * 6 * 6 * n**3, 8 * n * n),
        name="factor",
    )(gram)


def finish_kernel(total_rows, gram_ref, product_ref, out_ref, work):
    inverse, _ = inverse_factor(gram_ref[...] / total_rows, work)
    out_ref[...] = mm_nt(product_ref[...], inverse)


def finish(gram, product, total_rows):
    n = gram.shape[0]
    return pl.pallas_call(
        functools.partial(finish_kernel, total_rows),
        out_shape=jax.ShapeDtypeStruct(product.shape, F32),
        in_specs=[VMEM, VMEM],
        out_specs=VMEM,
        scratch_shapes=[pltpu.VMEM((2, n, n), F32)],
        cost_estimate=cost(2 * 6 * 6 * n**3 + 12 * product.shape[0] * n * n, 8 * product.size),
        name="finish",
    )(gram, product)


def near_terms(shape, place, near_cols, tiles, near):
    blocks, sources, per_source, tile = shape

    def add(r, acc):
        for k, ref in near:
            first = (r * sources + (place[0] ^ k)) * per_source
            for n in range(per_source):
                start = pl.multiple_of(near_cols[first + n] * tile, tile)
                part = jnp.dot(tiles[first + n], ref[pl.ds(start, tile), :], preferred_element_type=F32)
                acc = part if acc is None else acc + part
        return acc

    return add


def early_kernel(shape, n_near, groups, place, near_cols, far_groups, need, *refs):
    blocks, sources, per_source, tile = shape
    near = list(enumerate_sources(sources))[:n_near]
    near = list(zip(near, refs[:n_near]))
    far = refs[n_near : n_near + groups - 1]
    tiles_near, tiles_far, out_ref, table = refs[n_near + groups - 1 :]
    far_each = tiles_far.shape[0] // blocks
    for k in range(1, groups):
        h = place[1] ^ k
        start = pl.multiple_of(jnp.maximum(need[h], 0) * tile, tile)
        table[h] = far[k - 1][pl.ds(start, tile), :]
    add = near_terms(shape, place, near_cols, tiles_near, near)
    for r in range(blocks):
        acc = add(r, None)
        for t in range(r * far_each, (r + 1) * far_each):
            acc = acc + jnp.dot(tiles_far[t], table[far_groups[t]], preferred_element_type=F32)
        out_ref[pl.ds(r * tile, tile), :] = acc


def enumerate_sources(sources):
    order = [0]
    step = sources // 2
    while step:
        order += [k | step for k in order]
        step //= 2
    return order


def early(shape, groups, scalars, near, far, tiles_near, tiles_far):
    blocks, sources, per_source, tile = shape
    width = near[0].shape[1]
    count = len(near) * blocks * per_source + tiles_far.shape[0]
    return pl.pallas_call(
        functools.partial(early_kernel, shape, len(near), groups),
        out_shape=jax.ShapeDtypeStruct((blocks * tile, width), F32),
        in_specs=[SMEM] * 4 + [VMEM] * (len(near) + len(far) + 2),
        out_specs=VMEM,
        scratch_shapes=[pltpu.VMEM((groups, tile, width), BF16)],
        cost_estimate=cost(2 * count * tile * tile * width, 2 * count * tile * tile),
        compiler_params=pltpu.CompilerParams(vmem_limit_bytes=40 << 20),
        name="early",
    )(*scalars, *near, *far, tiles_near, tiles_far)


def late_rows(shape, place, near_cols, partial, late, tiles, r):
    blocks, sources, per_source, tile = shape
    order = enumerate_sources(sources)
    near = list(zip(order[len(order) - len(late) :], late))
    return near_terms(shape, place, near_cols, tiles, near)(r, partial[pl.ds(r * tile, tile), :])


def late_kernel(shape, n_late, place, near_cols, partial, *refs):
    late, (tiles, product_ref, rounded_ref, gram_ref) = refs[:n_late], refs[n_late:]
    blocks, _, _, tile = shape
    gram = None
    for r in range(blocks):
        acc = late_rows(shape, place, near_cols, partial, late, tiles, r)
        product_ref[pl.ds(r * tile, tile), :] = acc
        rounded_ref[pl.ds(r * tile, tile), :] = acc.astype(BF16)
        part = mm_tn(acc, acc)
        gram = part if gram is None else gram + part
    gram_ref[...] = gram


def late_scaled_kernel(shape, n_late, place, near_cols, partial, *refs):
    late, (tiles, inverse_ref, product_ref, gram_ref) = refs[:n_late], refs[n_late:]
    blocks, _, _, tile = shape
    gram = None
    for r in range(blocks):
        acc = late_rows(shape, place, near_cols, partial, late, tiles, r)
        acc = mm_nt(acc, inverse_ref[...])
        product_ref[pl.ds(r * tile, tile), :] = acc
        part = mm_tn(acc, acc)
        gram = part if gram is None else gram + part
    gram_ref[...] = gram


def late(shape, scalars, partial, rows, tiles, inverse=None):
    blocks, sources, per_source, tile = shape
    width = partial.shape[1]
    count = len(rows) * blocks * per_source
    wide = jax.ShapeDtypeStruct(partial.shape, F32)
    gram = jax.ShapeDtypeStruct((width, width), F32)
    if inverse is None:
        body, outs, more = late_kernel, (wide, jax.ShapeDtypeStruct(partial.shape, BF16), gram), ()
    else:
        body, outs, more = late_scaled_kernel, (wide, gram), (inverse,)
    return pl.pallas_call(
        functools.partial(body, shape, len(rows)),
        out_shape=outs,
        in_specs=[SMEM] * 2 + [VMEM] * (len(rows) + 2 + len(more)),
        out_specs=(VMEM,) * len(outs),
        cost_estimate=cost(2 * count * tile * tile * width + 12 * partial.size * width, 2 * count * tile * tile),
        compiler_params=pltpu.CompilerParams(vmem_limit_bytes=40 << 20),
        name="late",
    )(*scalars[:2], partial, *rows, tiles, *more)


def swap(x, axis, mask):
    size = lax.axis_size(axis)
    return lax.ppermute(x, axis, [(i, i ^ mask) for i in range(size)])


def near_rows(rows):
    held = [rows]
    step = lax.axis_size("blk") // 2
    while step:
        held += [swap(x, "blk", step) for x in held]
        step //= 2
    return held


def far_rows(rows):
    held = {0: rows}
    size = lax.axis_size("grp")
    for k in range(2, size, 2):
        held[k] = swap(rows, "grp", k)
    for k in range(1, size, 2):
        held[k] = swap(held[k - 1], "grp", 1)
    return [held[k] for k in range(1, size)]


def pair_sum(parts):
    while len(parts) > 1:
        parts = [a + b for a, b in zip(parts[::2], parts[1::2])]
    return parts[0]


def everywhere(x):
    x = x + swap(x, "grp", 1)
    x = pair_sum([x] + [swap(x, "grp", k) for k in range(2, lax.axis_size("grp"), 2)])
    return pair_sum([x] + [swap(x, "blk", k) for k in range(1, lax.axis_size("blk"))])


def per_device(tiles_near, near_cols, tiles_far, far_groups, need_blocks, start_vectors):
    tile = tiles_near.shape[1]
    blocks = start_vectors.shape[0] // tile
    sources = lax.axis_size("blk")
    groups = lax.axis_size("grp")
    shape = (blocks, sources, tiles_near.shape[0] // (blocks * sources), tile)
    total_rows = start_vectors.shape[0] * sources * groups
    place = jnp.stack([lax.axis_index("blk"), lax.axis_index("grp")]).astype(jnp.int32)
    scalars = (place, near_cols.reshape(-1), far_groups.reshape(-1), need_blocks.reshape(-1))
    split = 3 * sources // 4

    def gathered(rows):
        near, far = near_rows(rows), far_rows(rows)
        return early(shape, groups, scalars, near[:split], far, tiles_near, tiles_far), near[split:]

    partial, rest = gathered(start_vectors)
    product, rounded, gram = late(shape, scalars, partial, rest, tiles_near)
    for _ in range(ITERS - 1):
        inverse, fine = factor(everywhere(gram), total_rows)

        partial, rest = gathered(rounded)

        def quick(product, inverse, partial, rest):
            return late(shape, scalars, partial, rest, tiles_near, inverse)

        def plain(product, inverse, partial, rest):
            current = lax.dot_general(
                product, inverse, (((1,), (1,)), ((), ())), precision=HIGHEST, preferred_element_type=F32
            ).astype(BF16)
            partial, rest = gathered(current)
            product, _, gram = late(shape, scalars, partial, rest, tiles_near)
            return product, gram

        product, gram = lax.cond(fine[0] > 0, quick, plain, product, inverse, partial, rest)
        rounded = product.astype(BF16)
    return finish(everywhere(gram), product, total_rows)


def solution(mesh):
    in_specs = (
        P(AXES, None, None),
        P(AXES, None),
        P(AXES, None, None),
        P(AXES, None),
        P(AXES, None),
        P(AXES, None),
    )
    return jax.shard_map(
        per_device, mesh=mesh, in_specs=in_specs, out_specs=P(AXES, None), check_vma=False
    )
```

```python
import functools

import jax
import jax.numpy as jnp
from jax import lax
from jax.experimental import pallas as pl
from jax.experimental.pallas import tpu as pltpu
from jax.sharding import PartitionSpec as P

AXES = ("grp", "blk")
HIGHEST = lax.Precision.HIGHEST
INFLATION_MAX = 1.05
CORRECTION_MAX = 4e-6
VMEM = pl.BlockSpec(memory_space=pltpu.VMEM)
SMEM = pl.BlockSpec(memory_space=pltpu.SMEM)
ANY = pl.BlockSpec(memory_space=pl.ANY)
F32 = jnp.float32
NEED_ROWS = 16
DIAGONAL_ROWS = 8
BF16 = jnp.bfloat16
NN = (((1,), (0,)), ((), ()))
NT = (((1,), (1,)), ((), ()))
TN = (((0,), (0,)), ((), ()))


def cost(flops, nbytes):
    return pl.CostEstimate(flops=int(flops), bytes_accessed=int(nbytes), transcendentals=0)


def vmem(nbytes):
    return pltpu.CompilerParams(vmem_limit_bytes=int(nbytes) + (8 << 20))


def parts(x):
    high = x.astype(BF16)
    return high, (x - high.astype(F32)).astype(BF16)


def dot1(a, b, dims=NN):
    return lax.dot_general(a.astype(BF16), b.astype(BF16), dims, preferred_element_type=F32)


def dot3(a, b, dims=NN):
    a_high, a_low = parts(a)
    b_high, b_low = parts(b)
    return dot1(a_high, b_high, dims) + (dot1(a_high, b_low, dims) + dot1(a_low, b_high, dims))


def dot6(a, b, dims=NN):
    return lax.dot_general(a, b, dims, precision=HIGHEST, preferred_element_type=F32)


def inverse_factor(gram, work):
    n = gram.shape[0]
    rows = lax.broadcasted_iota(jnp.int32, (n, n), 0)
    cols = lax.broadcasted_iota(jnp.int32, (n, n), 1)
    on_diag = rows == cols
    eye = on_diag.astype(F32)
    weight = jnp.where(rows > cols, 1.0, jnp.where(on_diag, 0.5, 0.0)).astype(F32)
    diag = jnp.where(on_diag, gram, 0.0)
    scale_row = lax.rsqrt(jnp.sum(diag, axis=0, keepdims=True))
    scale_col = lax.rsqrt(jnp.sum(diag, axis=1, keepdims=True))
    base = gram * scale_col * scale_row - eye
    low = weight * base
    for dot in (dot1, dot3):
        moved = dot(low, base)
        crossed = dot(low + moved - base, low, NT)
        step = weight * (base - low - moved + crossed - low * eye)
        low = low + step - dot1(step, low)
    close = jnp.sum(step * step) <= CORRECTION_MAX
    work[0] = low

    @pl.when(jnp.logical_not(close))
    def _():
        work[0] = eye
        work[1] = base + eye

        def eliminate(j, carry):
            left = work[1]
            pivot_row = work[1, pl.ds(j, 1), :]
            pivot = jnp.sum(jnp.where(cols[:1] == j, pivot_row, 0.0), axis=1, keepdims=True)
            column = jnp.sum(jnp.where(cols == j, left, 0.0), axis=1, keepdims=True)
            factor = jnp.where(rows[:, :1] > j, column / pivot, 0.0)
            right_row = work[0, pl.ds(j, 1), :]
            work[1] = left - factor * pivot_row
            work[0] = work[0] - factor * right_row
            work[0, pl.ds(j, 1), :] = right_row * lax.rsqrt(pivot)
            return carry

        lax.fori_loop(0, n, eliminate, 0)
        work[0] = eye - work[0]

    return scale_row, close


def masks(n):
    rows = lax.broadcasted_iota(jnp.int32, (n, n), 0)
    cols = lax.broadcasted_iota(jnp.int32, (n, n), 1)
    return rows > cols, rows == cols


def halved(place, a, b, whole, mine, other):
    n = whole.shape[0]
    half = n // 2
    below, diagonal = masks(n)
    whole[...] = jnp.where(jnp.logical_or(below, diagonal), b, a)
    row = jnp.sum(jnp.where(diagonal, a, 0.0), axis=0, keepdims=True)
    here = pl.multiple_of((place[1] & 1) * half, half)
    for ref, start in ((mine, here), (other, half - here)):
        ref[:half, :] = whole[pl.ds(start, half), :]
        ref[half:, :] = jnp.broadcast_to(row, (DIAGONAL_ROWS, n))


def unhalved(place, mine, other, whole):
    n = whole.shape[0]
    half = n // 2
    here = pl.multiple_of((place[1] & 1) * half, half)
    whole[pl.ds(here, half), :] = mine[:half, :]
    whole[pl.ds(half - here, half), :] = other[:half, :]
    stored = whole[...]
    turned = stored.T
    below, diagonal = masks(n)
    a = jnp.where(diagonal, mine[half : half + 1, :], jnp.where(below, turned, stored))
    return a, jnp.where(jnp.logical_or(below, diagonal), stored, turned)


def scaled(x, scale, low, dot):
    x = x * scale
    return x - dot(x, low, NT)


def factors_kernel(total_rows, place, mine, other, low_ref, scale_ref, both_low_ref, both_scale_ref, flags, whole, work):
    n = whole.shape[0]
    _, on_diag = masks(n)
    first, second = unhalved(place, mine, other, whole)
    scale, close = inverse_factor(first / total_rows, work)
    low = work[0]
    low_ref[...] = low
    scale_ref[...] = scale
    inverse = on_diag.astype(F32) - low
    inflation = jnp.sum(inverse * inverse) / n
    flags[0] = jnp.logical_and(close, inflation <= INFLATION_MAX).astype(jnp.int32)
    scale_col = jnp.sum(jnp.where(on_diag, scale, 0.0), axis=1, keepdims=True)
    raw = second / total_rows * scale * scale_col
    raw = raw - dot3(low, raw)
    raw = raw - dot3(raw, low, NT)
    next_scale, next_close = inverse_factor(raw, work)
    next_low = work[0]
    flags[1] = next_close.astype(jnp.int32)
    next_col = jnp.sum(jnp.where(on_diag, next_scale, 0.0), axis=1, keepdims=True)
    moved = next_col * low
    both_low_ref[...] = moved + next_low * next_scale - dot3(next_low, moved)
    both_scale_ref[...] = next_scale


def factors(place, halves, total_rows):
    n = halves[0].shape[1]
    square, row = jax.ShapeDtypeStruct((n, n), F32), jax.ShapeDtypeStruct((1, n), F32)
    return pl.pallas_call(
        functools.partial(factors_kernel, total_rows),
        out_shape=(square, row, square, row, jax.ShapeDtypeStruct((2,), jnp.int32)),
        in_specs=[SMEM, VMEM, VMEM],
        out_specs=(VMEM, VMEM, VMEM, VMEM, SMEM),
        scratch_shapes=[pltpu.VMEM((n, n), F32), pltpu.VMEM((2, n, n), F32)],
        cost_estimate=cost(60 * n**3, 8 * n * n),
        compiler_params=vmem(0),
        name="factors",
    )(place, *halves)


def finish_kernel(flags, product, scale, low, next_scale, out_ref, done, sems):
    step = product.shape[0] // sems.shape[0]
    copies = []

    def write(dot, here):
        x = product[here, :] * scale[...]
        done[here, :] = x * next_scale[...] - dot(x, low[...], NT)

    for i in range(sems.shape[0]):
        here = pl.ds(i * step, step)
        pl.when(flags[1] > 0)(functools.partial(write, dot3, here))
        pl.when(flags[1] <= 0)(functools.partial(write, dot6, here))
        copies.append(pltpu.make_async_copy(done.at[here, :], out_ref.at[here, :], sems.at[i]))
        copies[-1].start()
    for copy in copies:
        copy.wait()


def finish(flags, product, scale, low, next_scale):
    return pl.pallas_call(
        finish_kernel,
        out_shape=pltpu.HBM(product.shape, F32),
        in_specs=[SMEM] + [VMEM] * 4,
        out_specs=ANY,
        scratch_shapes=[pltpu.VMEM(product.shape, F32), pltpu.SemaphoreType.DMA((4,))],
        cost_estimate=cost(6 * product.size * product.shape[1], 8 * product.size),
        compiler_params=vmem(4 * product.size),
        name="finish",
    )(flags, *held(product, scale, low, next_scale))


def with_tables(near, refs):
    out, used = [], 0
    spare = list(refs[sum(n for _, n in near) :])
    for k, n in near:
        chunks, used = refs[used : used + n], used + n
        table = chunks[0]
        if n > 1:
            table, rows = spare.pop(0), chunks[0].shape[0]
            for i, chunk in enumerate(chunks):
                table[pl.ds(i * rows, rows), :] = chunk[...]
        out.append((k, table))
    return out


def tables(near):
    rows = [sum(c.shape[0] for c in chunks) for _, chunks in near if len(chunks) > 1]
    return [pltpu.VMEM((n, near[0][1][0].shape[1]), BF16) for n in rows]


def counts(near):
    return [(k, len(chunks)) for k, chunks in near]


def flat(near):
    return [chunk for _, chunks in near for chunk in chunks]


def add_near(shape, place, near_cols, tiles, near, r, acc):
    blocks, sources, per_source, tile = shape
    for k, ref in near:
        first = (r * sources + (place[0] ^ k)) * per_source
        for n in range(per_source):
            start = pl.multiple_of(near_cols[first + n] * tile, tile)
            part = jnp.dot(tiles[first + n], ref[pl.ds(start, tile), :], preferred_element_type=F32)
            acc = part if acc is None else acc + part
    return acc


def load_kernel(n, *refs):
    ins, outs, sems = refs[:n], refs[-n - 1 : -1], refs[-1]
    copies = [pltpu.make_async_copy(ins[i], outs[i], sems.at[i]) for i in range(n)]
    for copy in copies:
        copy.start()
    for copy in copies:
        copy.wait()


def load(token, *arrays):
    n = len(arrays)
    return pl.pallas_call(
        functools.partial(load_kernel, n),
        out_shape=tuple(pltpu.VMEM(a.shape, a.dtype) for a in arrays),
        in_specs=[ANY] * (n + 1),
        out_specs=(VMEM,) * n,
        scratch_shapes=[pltpu.SemaphoreType.DMA((n,))],
        cost_estimate=cost(0, sum(a.size * 4 for a in arrays)),
        compiler_params=vmem(0),
        name="load",
    )(*outside(*arrays), token)


def outside(*arrays):
    return [pltpu.with_memory_space_constraint(a, pltpu.HBM) for a in arrays]


def held(*arrays):
    return [pltpu.with_memory_space_constraint(a, pltpu.VMEM) for a in arrays]


def relay_kernel(x_ref, *refs):
    refs[-1][...] = x_ref[...]


def relay(x, *tokens):
    return pl.pallas_call(
        relay_kernel,
        out_shape=pltpu.VMEM(x.shape, x.dtype),
        in_specs=[VMEM] + [ANY] * len(tokens),
        out_specs=VMEM,
        cost_estimate=cost(0, 0),
        compiler_params=vmem(0),
        name="relay",
    )(*held(x), *tokens)


def prepare_kernel(rows, need, out_ref):
    n, width = rows.shape
    out_ref[:n, :] = rows[...]
    lanes = lax.broadcasted_iota(jnp.int32, (NEED_ROWS, width), 1)
    needs = jnp.zeros((NEED_ROWS, width), F32)
    for h in range(need.shape[0]):
        needs = jnp.where(lanes == h, need[h].astype(F32), needs)
    out_ref[n:, :] = needs.astype(BF16)


def prepare(rows, need):
    n, width = rows.shape
    return pl.pallas_call(
        prepare_kernel,
        out_shape=pltpu.VMEM((n + NEED_ROWS, width), BF16),
        in_specs=[VMEM, SMEM],
        out_specs=VMEM,
        cost_estimate=cost(0, 0),
        compiler_params=vmem(4 * rows.size),
        name="prepare",
    )(rows, need)


def pack_kernel(tile, n, place, wanted, *refs):
    out_ref = refs[-1]
    size = tile + NEED_ROWS
    for i, ref in enumerate(refs[:n]):
        start = pl.multiple_of(jnp.maximum(wanted[place[1] ^ (2 * i)], 0) * tile, tile)
        out_ref[i * size : i * size + tile, :] = ref[pl.ds(start, tile), :]
        out_ref[i * size + tile : (i + 1) * size, :] = ref[ref.shape[0] - NEED_ROWS :, :]


def pack(tile, place, wanted, rows, tokens):
    return pl.pallas_call(
        functools.partial(pack_kernel, tile, len(rows)),
        out_shape=pltpu.VMEM((len(rows) * (tile + NEED_ROWS), rows[0].shape[1]), BF16),
        in_specs=[SMEM] * 2 + [VMEM] * len(rows) + [ANY] * len(tokens),
        out_specs=VMEM,
        cost_estimate=cost(0, 0),
        compiler_params=vmem(0),
        name="pack",
    )(place, wanted, *held(*rows), *tokens)


def core_pack_kernel(tile, own, *refs):
    out_ref = refs[-1]
    out_ref[:tile, :] = own[...]
    for i, ref in enumerate(refs[:-1], 1):
        out_ref[i * tile : (i + 1) * tile, :] = ref[tile:, :]


def core_pack(own, received):
    tile, width = own.shape
    n = 1 + len(received)
    return pl.pallas_call(
        functools.partial(core_pack_kernel, tile),
        out_shape=pltpu.VMEM((n * tile, width), BF16),
        in_specs=[VMEM] * n,
        out_specs=VMEM,
        cost_estimate=cost(0, 0),
        compiler_params=vmem(0),
        name="core_pack",
    )(*held(own, *received))


def near_kernel(shape, near, place, near_cols, *refs):
    blocks, _, _, tile = shape
    n = sum(count for _, count in near)
    tiles, out_ref = refs[n : n + 2]
    near_tables = with_tables(near, (*refs[:n], *refs[n + 2 :]))
    for r in range(blocks):
        out_ref[pl.ds(r * tile, tile), :] = add_near(shape, place, near_cols, tiles, near_tables, r, None)


def near_product(shape, scalars, near, tiles):
    blocks, _, _, tile = shape
    rows = flat(near)
    return pl.pallas_call(
        functools.partial(near_kernel, shape, counts(near)),
        out_shape=pltpu.VMEM((blocks * tile, rows[0].shape[1]), F32),
        in_specs=[SMEM] * 2 + [VMEM] * (len(rows) + 1),
        out_specs=VMEM,
        scratch_shapes=tables(near),
        cost_estimate=cost(0, 0),
        compiler_params=vmem(0),
        name="near",
    )(*scalars[:2], *held(*rows, tiles))


def far_table(place, need, far, packed, table):
    tile = table.shape[1]
    size = tile + NEED_ROWS
    for i in range(len(far) + 1):
        h = place[1] ^ (2 * i)
        table[h ^ 1] = packed[i * size : i * size + tile, :]
        if i:
            start = pl.multiple_of(jnp.maximum(need[h], 0) * tile, tile)
            table[h] = far[i - 1][pl.ds(start, tile), :]


def add_far(far_groups, tiles, table, r, blocks, acc):
    each = tiles.shape[0] // blocks
    for t in range(r * each, (r + 1) * each):
        acc = acc + jnp.dot(tiles[t], table[far_groups[t]], preferred_element_type=F32)
    return acc


def gram_of(rows, tile):
    gram = None
    for start in range(0, rows.shape[0], tile):
        both = jnp.concatenate(parts(rows[pl.ds(start, tile), :]), axis=1)
        part = lax.dot_general(both, both, TN, preferred_element_type=F32)
        gram = part if gram is None else gram + part
    n = rows.shape[1]
    crossed = gram[:n, n:]
    return gram[:n, :n] + (crossed + crossed.T) + gram[n:, n:]


def late_kernel(shape, place, far_groups, need, partial, *refs):
    blocks, _, _, tile = shape
    *far, packed, tiles = refs[: need.shape[0] // 2 + 1]
    product_ref, rounded_ref, first_ref, second_ref, table = refs[need.shape[0] // 2 + 1 :]
    far_table(place, need, far, packed, table)
    for r in range(blocks):
        here = pl.ds(r * tile, tile)
        acc = add_far(far_groups, tiles, table, r, blocks, partial[here, :])
        product_ref[here, :] = acc
        rounded_ref[here, :] = acc.astype(BF16)
        half_ref, q = (first_ref, r) if r < blocks // 2 else (second_ref, r - blocks // 2)
        half_ref[pl.ds(q * tile, tile), :] = acc.astype(BF16)


def late(shape, scalars, need, partial, far, tiles):
    n, width = partial.shape
    groups, (blocks, _, _, tile) = need.shape[0], shape
    half = pltpu.VMEM((n // 2, width), BF16)
    return pl.pallas_call(
        functools.partial(late_kernel, shape),
        out_shape=(pltpu.VMEM((n, width), F32), pltpu.VMEM((n, width), BF16), half, half),
        in_specs=[SMEM] * 3 + [VMEM] * (len(far) + 2),
        out_specs=(VMEM,) * 4,
        scratch_shapes=[pltpu.VMEM((groups, tile, width), BF16)],
        cost_estimate=cost(0, 0),
        compiler_params=vmem(0),
        name="late",
    )(scalars[0], scalars[2], need, *held(partial, *far, tiles))


def gram_kernel(tile, product, out_ref):
    out_ref[...] = gram_of(product, tile)


def gram(tile, product):
    width = product.shape[1]
    return pl.pallas_call(
        functools.partial(gram_kernel, tile),
        out_shape=pltpu.VMEM((width, width), F32),
        in_specs=[VMEM],
        out_specs=VMEM,
        cost_estimate=cost(0, 0),
        compiler_params=vmem(0),
        name="gram",
    )(*held(product))


def halves_kernel(place, a, b, mine, other, whole):
    halved(place, a[...], b[...], whole, mine, other)


def halves_of(place, a, b):
    n = a.shape[0]
    half = pltpu.VMEM((n // 2 + DIAGONAL_ROWS, n), F32)
    return pl.pallas_call(
        halves_kernel,
        out_shape=(half, half),
        in_specs=[SMEM] + [VMEM] * 2,
        out_specs=(VMEM,) * 2,
        scratch_shapes=[pltpu.VMEM((n, n), F32)],
        compiler_params=vmem(0),
        name="halves",
    )(place, a, b)


def blocks_kernel(tile, n_far, place, rounded, *refs):
    *far, packed = refs[:n_far]
    own_ref, *outs = refs[n_far + 1 :]
    lane = lax.broadcasted_iota(jnp.int32, (1, rounded.shape[1]), 1) == place[1]
    size = tile + NEED_ROWS

    def wanted_block(k):
        ref, first = (packed, k // 2 * size + tile) if k % 2 else (far[k // 2 - 1], far[0].shape[0] - NEED_ROWS)
        needs = ref[first : first + NEED_ROWS, :].astype(F32)[:1]
        block = jnp.maximum(jnp.sum(jnp.where(lane, needs, 0.0)).astype(jnp.int32), 0)
        return rounded[pl.ds(pl.multiple_of(block * tile, tile), tile), :]

    own_ref[...] = wanted_block(1)
    for i, out_ref in enumerate(outs, 1):
        out_ref[:tile, :] = wanted_block(2 * i)
        out_ref[tile:, :] = wanted_block(2 * i + 1)


def blocks_for_others(tile, place, rounded, far, token):
    width = rounded.shape[1]
    pair = pltpu.VMEM((2 * tile, width), BF16)
    return pl.pallas_call(
        functools.partial(blocks_kernel, tile, len(far)),
        out_shape=(pltpu.VMEM((tile, width), BF16), *(pair,) * (len(far) - 1)),
        in_specs=[SMEM] + [VMEM] * (1 + len(far)) + [ANY],
        out_specs=(VMEM,) * len(far),
        cost_estimate=cost(0, 0),
        compiler_params=vmem(0),
        name="blocks",
    )(place, *held(rounded, *far), token)


def last_kernel(shape, near, n_far, place, near_cols, far_groups, partial, *refs):
    blocks, _, _, tile = shape
    n = sum(count for _, count in near)
    packed, far = refs[n], refs[n + 1 : n + n_far]
    refs = (*refs[:n], *refs[n + n_far :])
    past, tiles_near, tiles_far, product_ref, mine, other, whole, table = refs[n : n + 8]
    near_tables = with_tables(near, (*refs[:n], *refs[n + 8 :]))
    for i in range(len(far) + 1):
        table[place[1] ^ (2 * i + 1)] = packed[i * tile : (i + 1) * tile, :]
        if i:
            table[place[1] ^ (2 * i)] = far[i - 1][:tile, :]
    for r in range(blocks):
        here = pl.ds(r * tile, tile)
        acc = add_near(shape, place, near_cols, tiles_near, near_tables, r, partial[here, :])
        product_ref[here, :] = add_far(far_groups, tiles_far, table, r, blocks, acc)
    halved(place, past[...], gram_of(product_ref, tile), whole, mine, other)


def last(shape, groups, scalars, partial, near, far, tiles_near, tiles_far, past):
    rows = flat(near)
    width = partial.shape[1]
    half = pltpu.VMEM((width // 2 + DIAGONAL_ROWS, width), F32)
    return pl.pallas_call(
        functools.partial(last_kernel, shape, counts(near), len(far)),
        out_shape=(pltpu.VMEM(partial.shape, F32), half, half),
        in_specs=[SMEM] * 3 + [VMEM] * (len(rows) + len(far) + 4),
        out_specs=(VMEM,) * 3,
        scratch_shapes=[
            pltpu.VMEM((width, width), F32),
            pltpu.VMEM((groups, shape[3], width), BF16),
            *tables(near),
        ],
        cost_estimate=cost(0, 0),
        compiler_params=vmem(0),
        name="last",
    )(*scalars, *held(partial, *rows, *far, past, tiles_near, tiles_far))


def swap(x, axis, mask):
    size = lax.axis_size(axis)
    return lax.ppermute(x, axis, [(i, i ^ mask) for i in range(size)])


def near_rows(rows, chunks, tokens):
    step = lax.axis_size("blk") // 2
    here = [(0, [rows]), (step, [swap(x, "blk", step) for x in chunks])]
    while step > 1:
        step //= 2
        direct = swap(rows, "blk", step)
        moved = [(step, [direct])]
        for k, (*before, after) in here[1:]:
            sent = [swap(x, "blk", step) for x in before]
            sent.append(swap(relay(after, direct, *sent, *tokens), "blk", step))
            moved.append((k | step, sent))
        here += moved
    return here


def bits(size, scale):
    return [scale << i for i in range(size.bit_length() - 1)]


def everywhere(mine, other):
    positions = lax.axis_size("blk")
    chips, places = bits(lax.axis_size("grp"), positions)[1:], bits(positions, 1)
    x = mine + swap(other, "grp", 1)
    while chips or places:
        a, b = chips[:1], places[:1]
        chips, places = chips[1:], places[1:]
        if a and b:
            x = (x + swap(x, AXES, a[0])) + (swap(x, AXES, b[0]) + swap(x, AXES, a[0] | b[0]))
        else:
            x = x + swap(x, AXES, (a + b)[0])
    return x, swap(x, "grp", 1)


def per_device(tiles_near, near_cols, tiles_far, far_groups, need_blocks, start_vectors):
    tile = tiles_near.shape[1]
    blocks = start_vectors.shape[0] // tile
    sources = lax.axis_size("blk")
    groups = lax.axis_size("grp")
    shape = (blocks, sources, tiles_near.shape[0] // (blocks * sources), tile)
    total_rows = start_vectors.shape[0] * sources * groups
    place = jnp.stack([lax.axis_index("blk"), lax.axis_index("grp")]).astype(jnp.int32)
    scalars = (place, near_cols.reshape(-1), far_groups.reshape(-1))
    need = need_blocks.reshape(-1)
    wanted = swap(need_blocks, "grp", 1).reshape(-1)
    split = 3 * sources // 4

    def begin(rows):
        below = prepare(rows, need)
        far = [swap(below, "grp", k) for k in range(2, groups, 2)]
        near = near_rows(rows, [rows], ())
        near[0] = (0, [below])
        tiles = load(near[1][1][0], tiles_near, tiles_far)
        far.append(swap(pack(tile, place, wanted, [below, *far], [*near[-1][1], *tiles]), "grp", 1))
        partial = near_product(shape, scalars, near, tiles[0])
        return tiles, far, late(shape, scalars, need, partial, far, tiles[1])

    tiles, far, (product, rounded, first, second) = begin(start_vectors)
    past = gram(tile, product)
    own, *outs = blocks_for_others(tile, place, rounded, far, past)
    near = near_rows(rounded, [first, second], ())
    far = [swap(x, "grp", 2 * i) for i, x in enumerate(outs, 1)]
    far.insert(0, swap(core_pack(own, far), "grp", 1))
    partial = near_product(shape, scalars, near[:split], tiles[0])
    moved, *halves = last(shape, groups, scalars, partial, near[split:], far, *tiles, past)
    low, scale, both_low, next_scale, flags = factors(place, everywhere(*halves), total_rows)

    def quick(start, moved, low, scale, both_low, next_scale, flags):
        return finish(flags, moved, scale, both_low, next_scale)

    def plain(start, moved, low, scale, both_low, next_scale, flags):
        _, _, (product, *_) = begin(start)
        current = scaled(product, scale, low, dot6).astype(BF16)
        _, _, (product, *_) = begin(current)
        unit = jnp.eye(product.shape[1], dtype=F32) * start.shape[0]
        halves = everywhere(*halves_of(place, unit, gram(tile, product)))
        _, scale, both_low, next_scale, flags = factors(place, halves, total_rows)
        return finish(flags, product, scale, both_low, next_scale)

    return lax.cond(flags[0] > 0, quick, plain, start_vectors, moved, low, scale, both_low, next_scale, flags)


def solution(mesh):
    in_specs = (
        P(AXES, None, None),
        P(AXES, None),
        P(AXES, None, None),
        P(AXES, None),
        P(AXES, None),
        P(AXES, None),
    )
    return jax.shard_map(
        per_device, mesh=mesh, in_specs=in_specs, out_specs=P(AXES, None), check_vma=False
    )
```

```python
import functools

import jax
import jax.numpy as jnp
from jax import lax
from jax.experimental import pallas as pl
from jax.experimental.pallas import tpu as pltpu
from jax.sharding import PartitionSpec as P

AXES = ("grp", "blk")
HIGHEST = lax.Precision.HIGHEST
INFLATION_MAX = 1.15
CORRECTION_MAX = 4e-6
VMEM = pl.BlockSpec(memory_space=pltpu.VMEM)
SMEM = pl.BlockSpec(memory_space=pltpu.SMEM)
ANY = pl.BlockSpec(memory_space=pl.ANY)
F32 = jnp.float32
NEED_ROWS = 16
DIAGONAL_ROWS = 8
BF16 = jnp.bfloat16
NN = (((1,), (0,)), ((), ()))
NT = (((1,), (1,)), ((), ()))
TN = (((0,), (0,)), ((), ()))


def cost(flops, nbytes):
    return pl.CostEstimate(flops=int(flops), bytes_accessed=int(nbytes), transcendentals=0)


def vmem(nbytes):
    return pltpu.CompilerParams(vmem_limit_bytes=int(nbytes) + (8 << 20))


def parts(x):
    high = x.astype(BF16)
    return high, (x - high.astype(F32)).astype(BF16)


def dot1(a, b, dims=NN):
    return lax.dot_general(a.astype(BF16), b.astype(BF16), dims, preferred_element_type=F32)


def dot3(a, b, dims=NN):
    a_high, a_low = parts(a)
    b_high, b_low = parts(b)
    (across,), (down,) = dims[0]
    return dot1(jnp.concatenate([a_high, a_low, a_high], across), jnp.concatenate([b_high, b_high, b_low], down), dims)


def dot6(a, b, dims=NN):
    return lax.dot_general(a, b, dims, precision=HIGHEST, preferred_element_type=F32)


def normalised(gram):
    _, on_diag = masks(gram.shape[0])
    diag = jnp.where(on_diag, gram, 0.0)
    scale_row = lax.rsqrt(jnp.sum(diag, axis=0, keepdims=True))
    scale_col = lax.rsqrt(jnp.sum(diag, axis=1, keepdims=True))
    return scale_row, gram * scale_col * scale_row - on_diag.astype(F32)


def iterated(base):
    below, on_diag = masks(base.shape[0])
    eye = on_diag.astype(F32)
    weight = below.astype(F32) + 0.5 * eye
    first = weight * base
    moved = dot1(first, base)
    low = first + weight * (dot1(moved, first, NT) - moved) + dot1(weight * moved, first)
    moved = dot3(low, base)
    crossed = dot3(low + moved - base, low, NT)
    step = weight * (base - low - moved + crossed - low * eye)
    return low + step - dot1(step, low), jnp.sum(step * step)


def eliminated(base, work):
    n = base.shape[0]
    rows = lax.broadcasted_iota(jnp.int32, (n, n), 0)
    cols = lax.broadcasted_iota(jnp.int32, (n, n), 1)
    eye = (rows == cols).astype(F32)
    work[0] = eye
    work[1] = base + eye

    def eliminate(j, carry):
        left = work[1]
        pivot_row = work[1, pl.ds(j, 1), :]
        pivot = jnp.sum(jnp.where(cols[:1] == j, pivot_row, 0.0), axis=1, keepdims=True)
        column = jnp.sum(jnp.where(cols == j, left, 0.0), axis=1, keepdims=True)
        factor = jnp.where(rows[:, :1] > j, column / pivot, 0.0)
        right_row = work[0, pl.ds(j, 1), :]
        work[1] = left - factor * pivot_row
        work[0] = work[0] - factor * right_row
        work[0, pl.ds(j, 1), :] = right_row * lax.rsqrt(pivot)
        return carry

    lax.fori_loop(0, n, eliminate, 0)
    return eye - work[0]


def masks(n):
    rows = lax.broadcasted_iota(jnp.int32, (n, n), 0)
    cols = lax.broadcasted_iota(jnp.int32, (n, n), 1)
    return rows > cols, rows == cols


def halved(place, a, b, whole, mine, other):
    n = whole.shape[0]
    half = n // 2
    below, diagonal = masks(n)
    whole[...] = jnp.where(jnp.logical_or(below, diagonal), b, a)
    row = jnp.sum(jnp.where(diagonal, a, 0.0), axis=0, keepdims=True)
    here = pl.multiple_of((place[1] & 1) * half, half)
    for ref, start in ((mine, here), (other, half - here)):
        ref[:half, :] = whole[pl.ds(start, half), :]
        ref[half:, :] = jnp.broadcast_to(row, (DIAGONAL_ROWS, n))


def unhalved(place, mine, other, whole):
    n = whole.shape[0]
    half = n // 2
    here = pl.multiple_of((place[1] & 1) * half, half)
    whole[pl.ds(here, half), :] = mine[:half, :]
    whole[pl.ds(half - here, half), :] = other[:half, :]
    stored = whole[...]
    turned = stored.T
    below, diagonal = masks(n)
    a = jnp.where(diagonal, mine[half : half + 1, :], jnp.where(below, turned, stored))
    return a, jnp.where(jnp.logical_or(below, diagonal), stored, turned)


def scaled(x, scale, low, dot):
    x = x * scale
    return x - dot(x, low, NT)


def inflation_of(low):
    inverse = masks(low.shape[0])[1].astype(F32) - low
    return jnp.sum(inverse * inverse) / low.shape[0]


def both_factors(first, second, low_of, dot):
    _, on_diag = masks(first.shape[0])

    def as_column(row):
        return jnp.sum(jnp.where(on_diag, row, 0.0), axis=1, keepdims=True)

    scale, base = normalised(first)
    low = low_of(base)
    raw = second * scale * as_column(scale)
    raw = raw - dot(low, raw)
    raw = raw - dot(raw, low, NT)
    next_scale, base = normalised(raw)
    next_low = low_of(base)
    moved = as_column(next_scale) * low
    return low, scale, moved + next_low * next_scale - dot(next_low, moved), next_scale, next_low


def finish_kernel(total_rows, place, mine, other, product, out_ref, low_ref, scale_ref, fine_ref, whole, work, done, sems):
    first, second = [x / total_rows for x in unhalved(place, mine, other, whole)]
    step = product.shape[0] // sems.shape[0]
    sizes = []

    def quickly(base):
        low, size = iterated(base)
        sizes.append(size)
        return low

    def write(low, scale, both_low, next_scale, dot):
        low_ref[...] = low
        scale_ref[...] = scale
        copies = []
        for i in range(sems.shape[0]):
            here = pl.ds(i * step, step)
            x = product[here, :] * scale
            done[here, :] = x * next_scale - dot(x, both_low, NT)
            copies.append(pltpu.make_async_copy(done.at[here, :], out_ref.at[here, :], sems.at[i]))
            copies[-1].start()
        for copy in copies:
            copy.wait()

    *found, next_low = both_factors(first, second, quickly, dot3)
    write(*found, dot3)
    close = jnp.maximum(*sizes) <= CORRECTION_MAX
    fine = jnp.maximum(inflation_of(found[0]), inflation_of(next_low)) <= INFLATION_MAX
    fine_ref[0] = jnp.logical_and(close, fine).astype(jnp.int32)

    @pl.when(jnp.logical_not(close))
    def _():
        *found, _ = both_factors(first, second, lambda base: eliminated(base, work), dot6)
        write(*found, dot6)


def finish(place, halves, product, total_rows):
    n = product.shape[1]
    return pl.pallas_call(
        functools.partial(finish_kernel, total_rows),
        out_shape=(
            pltpu.HBM(product.shape, F32),
            jax.ShapeDtypeStruct((n, n), F32),
            jax.ShapeDtypeStruct((1, n), F32),
            jax.ShapeDtypeStruct((1,), jnp.int32),
        ),
        in_specs=[SMEM] + [VMEM] * 3,
        out_specs=(ANY, VMEM, VMEM, SMEM),
        scratch_shapes=[
            pltpu.VMEM((n, n), F32),
            pltpu.VMEM((2, n, n), F32),
            pltpu.VMEM(product.shape, F32),
            pltpu.SemaphoreType.DMA((4,)),
        ],
        cost_estimate=cost(60 * n**3 + 6 * product.size * n, 8 * product.size),
        compiler_params=vmem(8 * product.size),
        name="finish",
    )(place, *held(*halves, product))


def add_near(shape, place, near_cols, tiles, near, r, acc):
    blocks, sources, per_source, tile = shape
    for k, ref in near:
        first = (r * sources + (place[0] ^ k)) * per_source
        for n in range(per_source):
            start = pl.multiple_of(near_cols[first + n] * tile, tile)
            part = jnp.dot(tiles[first + n], ref[pl.ds(start, tile), :], preferred_element_type=F32)
            acc = part if acc is None else acc + part
    return acc


def load_kernel(n, *refs):
    ins, outs, sems = refs[:n], refs[-n - 1 : -1], refs[-1]
    copies = [pltpu.make_async_copy(ins[i], outs[i], sems.at[i]) for i in range(n)]
    for copy in copies:
        copy.start()
    for copy in copies:
        copy.wait()


def load(token, *arrays):
    n = len(arrays)
    return pl.pallas_call(
        functools.partial(load_kernel, n),
        out_shape=tuple(pltpu.VMEM(a.shape, a.dtype) for a in arrays),
        in_specs=[ANY] * (n + 1),
        out_specs=(VMEM,) * n,
        scratch_shapes=[pltpu.SemaphoreType.DMA((n,))],
        cost_estimate=cost(0, sum(a.size * 4 for a in arrays)),
        compiler_params=vmem(0),
        name="load",
    )(*outside(*arrays), token)


def outside(*arrays):
    return [pltpu.with_memory_space_constraint(a, pltpu.HBM) for a in arrays]


def held(*arrays):
    return [pltpu.with_memory_space_constraint(a, pltpu.VMEM) for a in arrays]


def relay_kernel(x_ref, *refs):
    refs[-1][...] = x_ref[...]


def relay(x, *tokens):
    return pl.pallas_call(
        relay_kernel,
        out_shape=pltpu.VMEM(x.shape, x.dtype),
        in_specs=[VMEM] + [ANY] * len(tokens),
        out_specs=VMEM,
        cost_estimate=cost(0, 0),
        compiler_params=vmem(0),
        name="relay",
    )(*held(x), *tokens)


def prepare_kernel(rows, need, out_ref):
    n, width = rows.shape
    out_ref[:n, :] = rows[...]
    lanes = lax.broadcasted_iota(jnp.int32, (NEED_ROWS, width), 1)
    needs = jnp.zeros((NEED_ROWS, width), F32)
    for h in range(need.shape[0]):
        needs = jnp.where(lanes == h, need[h].astype(F32), needs)
    out_ref[n:, :] = needs.astype(BF16)


def prepare(rows, need):
    n, width = rows.shape
    return pl.pallas_call(
        prepare_kernel,
        out_shape=pltpu.VMEM((n + NEED_ROWS, width), BF16),
        in_specs=[VMEM, SMEM],
        out_specs=VMEM,
        cost_estimate=cost(0, 0),
        compiler_params=vmem(4 * rows.size),
        name="prepare",
    )(rows, need)


def pack_kernel(tile, n, place, wanted, *refs):
    out_ref = refs[-1]
    size = tile + NEED_ROWS
    for i, ref in enumerate(refs[:n]):
        start = pl.multiple_of(jnp.maximum(wanted[place[1] ^ (2 * i)], 0) * tile, tile)
        out_ref[i * size : i * size + tile, :] = ref[pl.ds(start, tile), :]
        out_ref[i * size + tile : (i + 1) * size, :] = ref[ref.shape[0] - NEED_ROWS :, :]


def pack(tile, place, wanted, rows, tokens):
    return pl.pallas_call(
        functools.partial(pack_kernel, tile, len(rows)),
        out_shape=pltpu.VMEM((len(rows) * (tile + NEED_ROWS), rows[0].shape[1]), BF16),
        in_specs=[SMEM] * 2 + [VMEM] * len(rows) + [ANY] * len(tokens),
        out_specs=VMEM,
        cost_estimate=cost(0, 0),
        compiler_params=vmem(0),
        name="pack",
    )(place, wanted, *held(*rows), *tokens)


def core_pack_kernel(tile, own, *refs):
    out_ref = refs[-1]
    out_ref[:tile, :] = own[...]
    for i, ref in enumerate(refs[:-1], 1):
        out_ref[i * tile : (i + 1) * tile, :] = ref[tile:, :]


def core_pack(own, received):
    tile, width = own.shape
    n = 1 + len(received)
    return pl.pallas_call(
        functools.partial(core_pack_kernel, tile),
        out_shape=pltpu.VMEM((n * tile, width), BF16),
        in_specs=[VMEM] * n,
        out_specs=VMEM,
        cost_estimate=cost(0, 0),
        compiler_params=vmem(0),
        name="core_pack",
    )(*held(own, *received))


def early_kernel(shape, distances, n_far, place, near_cols, far_groups, *refs):
    blocks, _, _, tile = shape
    n = len(distances)
    near = list(zip(distances, refs[:n]))
    packed, far = refs[n], refs[n + 1 : n + n_far]
    tiles_near, tiles_far, out_ref, table = refs[n + n_far :]
    for i in range(len(far) + 1):
        table[place[1] ^ (2 * i + 1)] = packed[i * tile : (i + 1) * tile, :]
        if i:
            table[place[1] ^ (2 * i)] = far[i - 1][:tile, :]
    for r in range(blocks):
        here = pl.ds(r * tile, tile)
        acc = add_near(shape, place, near_cols, tiles_near, near, r, None)
        out_ref[here, :] = add_far(far_groups, tiles_far, table, r, blocks, acc)


def early(shape, groups, scalars, near, far, tiles_near, tiles_far):
    blocks, _, _, tile = shape
    distances, rows = zip(*near)
    width = rows[0].shape[1]
    return pl.pallas_call(
        functools.partial(early_kernel, shape, distances, len(far)),
        out_shape=pltpu.VMEM((blocks * tile, width), F32),
        in_specs=[SMEM] * 3 + [VMEM] * (len(rows) + len(far) + 2),
        out_specs=VMEM,
        scratch_shapes=[pltpu.VMEM((groups, tile, width), BF16)],
        cost_estimate=cost(0, 0),
        compiler_params=vmem(0),
        name="early",
    )(*scalars, *held(*rows, *far, tiles_near, tiles_far))


def near_kernel(shape, distances, place, near_cols, *refs):
    blocks, _, _, tile = shape
    n = len(distances)
    *before, tiles, out_ref = refs[n:]
    near = list(zip(distances, refs[:n]))
    for r in range(blocks):
        here = pl.ds(r * tile, tile)
        acc = before[0][here, :] if before else None
        out_ref[here, :] = add_near(shape, place, near_cols, tiles, near, r, acc)


def near_product(shape, scalars, near, tiles, *before):
    blocks, _, _, tile = shape
    distances, rows = zip(*near)
    return pl.pallas_call(
        functools.partial(near_kernel, shape, distances),
        out_shape=pltpu.VMEM((blocks * tile, rows[0].shape[1]), F32),
        in_specs=[SMEM] * 2 + [VMEM] * (len(rows) + len(before) + 1),
        out_specs=VMEM,
        cost_estimate=cost(0, 0),
        compiler_params=vmem(0),
        name="near",
    )(*scalars[:2], *held(*rows, *before, tiles))


def far_table(place, need, far, packed, table):
    tile = table.shape[1]
    size = tile + NEED_ROWS
    for i in range(len(far) + 1):
        h = place[1] ^ (2 * i)
        table[h ^ 1] = packed[i * size : i * size + tile, :]
        if i:
            start = pl.multiple_of(jnp.maximum(need[h], 0) * tile, tile)
            table[h] = far[i - 1][pl.ds(start, tile), :]


def add_far(far_groups, tiles, table, r, blocks, acc):
    each = tiles.shape[0] // blocks
    for t in range(r * each, (r + 1) * each):
        acc = acc + jnp.dot(tiles[t], table[far_groups[t]], preferred_element_type=F32)
    return acc


def gram_of(rows, tile):
    gram = None
    for start in range(0, rows.shape[0], tile):
        both = jnp.concatenate(parts(rows[pl.ds(start, tile), :]), axis=1)
        part = lax.dot_general(both, both, TN, preferred_element_type=F32)
        gram = part if gram is None else gram + part
    n = rows.shape[1]
    crossed = gram[:n, n:]
    return gram[:n, :n] + (crossed + crossed.T) + gram[n:, n:]


def late_kernel(shape, place, far_groups, need, partial, *refs):
    blocks, _, _, tile = shape
    *far, packed, tiles = refs[: need.shape[0] // 2 + 1]
    product_ref, rounded_ref, table = refs[need.shape[0] // 2 + 1 :]
    far_table(place, need, far, packed, table)
    for r in range(blocks):
        here = pl.ds(r * tile, tile)
        acc = add_far(far_groups, tiles, table, r, blocks, partial[here, :])
        product_ref[here, :] = acc
        rounded_ref[here, :] = acc.astype(BF16)


def late(shape, scalars, need, partial, far, tiles):
    n, width = partial.shape
    groups, tile = need.shape[0], shape[3]
    return pl.pallas_call(
        functools.partial(late_kernel, shape),
        out_shape=(pltpu.VMEM((n, width), F32), pltpu.VMEM((n, width), BF16)),
        in_specs=[SMEM] * 3 + [VMEM] * (len(far) + 2),
        out_specs=(VMEM,) * 2,
        scratch_shapes=[pltpu.VMEM((groups, tile, width), BF16)],
        cost_estimate=cost(0, 0),
        compiler_params=vmem(0),
        name="late",
    )(scalars[0], scalars[2], need, *held(partial, *far, tiles))


def gram_kernel(tile, product, rounded, out_ref, copy_ref):
    out_ref[...] = gram_of(product, tile)
    copy_ref[...] = rounded[...]


def gram(tile, product, rounded):
    width = product.shape[1]
    return pl.pallas_call(
        functools.partial(gram_kernel, tile),
        out_shape=(pltpu.VMEM((width, width), F32), pltpu.VMEM(rounded.shape, BF16)),
        in_specs=[VMEM] * 2,
        out_specs=(VMEM,) * 2,
        cost_estimate=cost(0, 0),
        compiler_params=vmem(0),
        name="gram",
    )(*held(product, rounded))


def halves_kernel(place, a, b, mine, other, whole):
    halved(place, a[...], b[...], whole, mine, other)


def halves_of(place, a, b):
    n = a.shape[0]
    half = pltpu.VMEM((n // 2 + DIAGONAL_ROWS, n), F32)
    return pl.pallas_call(
        halves_kernel,
        out_shape=(half, half),
        in_specs=[SMEM] + [VMEM] * 2,
        out_specs=(VMEM,) * 2,
        scratch_shapes=[pltpu.VMEM((n, n), F32)],
        compiler_params=vmem(0),
        name="halves",
    )(place, a, b)


def blocks_kernel(tile, n_far, place, rounded, *refs):
    *far, packed = refs[:n_far]
    own_ref, *outs = refs[n_far + 1 :]
    lane = lax.broadcasted_iota(jnp.int32, (1, rounded.shape[1]), 1) == place[1]
    size = tile + NEED_ROWS

    def wanted_block(k):
        ref, first = (packed, k // 2 * size + tile) if k % 2 else (far[k // 2 - 1], far[0].shape[0] - NEED_ROWS)
        needs = ref[first : first + NEED_ROWS, :].astype(F32)[:1]
        block = jnp.maximum(jnp.sum(jnp.where(lane, needs, 0.0)).astype(jnp.int32), 0)
        return rounded[pl.ds(pl.multiple_of(block * tile, tile), tile), :]

    own_ref[...] = wanted_block(1)
    for i, out_ref in enumerate(outs, 1):
        out_ref[:tile, :] = wanted_block(2 * i)
        out_ref[tile:, :] = wanted_block(2 * i + 1)


def blocks_for_others(tile, place, rounded, far, token):
    width = rounded.shape[1]
    pair = pltpu.VMEM((2 * tile, width), BF16)
    return pl.pallas_call(
        functools.partial(blocks_kernel, tile, len(far)),
        out_shape=(pltpu.VMEM((tile, width), BF16), *(pair,) * (len(far) - 1)),
        in_specs=[SMEM] + [VMEM] * (1 + len(far)) + [ANY],
        out_specs=(VMEM,) * len(far),
        cost_estimate=cost(0, 0),
        compiler_params=vmem(0),
        name="blocks",
    )(place, *held(rounded, *far), token)


def last_kernel(shape, distances, place, near_cols, partial, *refs):
    blocks, _, _, tile = shape
    n = len(distances)
    near = list(zip(distances, refs[:n]))
    past, tiles, product_ref, mine, other, whole = refs[n:]
    for r in range(blocks):
        here = pl.ds(r * tile, tile)
        product_ref[here, :] = add_near(shape, place, near_cols, tiles, near, r, partial[here, :])
    halved(place, past[...], gram_of(product_ref, tile), whole, mine, other)


def last(shape, scalars, partial, near, tiles, past):
    distances, rows = zip(*near)
    width = partial.shape[1]
    half = pltpu.VMEM((width // 2 + DIAGONAL_ROWS, width), F32)
    return pl.pallas_call(
        functools.partial(last_kernel, shape, distances),
        out_shape=(pltpu.VMEM(partial.shape, F32), half, half),
        in_specs=[SMEM] * 2 + [VMEM] * (len(rows) + 3),
        out_specs=(VMEM,) * 3,
        scratch_shapes=[pltpu.VMEM((width, width), F32)],
        cost_estimate=cost(0, 0),
        compiler_params=vmem(0),
        name="last",
    )(*scalars[:2], *held(partial, *rows, past, tiles))


def swap(x, axis, mask):
    size = lax.axis_size(axis)
    return lax.ppermute(x, axis, [(i, i ^ mask) for i in range(size)])


def near_rows(rows, again):
    step = lax.axis_size("blk") // 2
    here = [(0, rows), (step, swap(rows, "blk", step))]
    while step > 1:
        step //= 2
        direct = swap(again, "blk", step)
        here += [(step, direct)] + [(k | step, swap(relay(x, direct), "blk", step)) for k, x in here[1:]]
    return here


def bits(size, scale):
    return [scale << i for i in range(size.bit_length() - 1)]


def everywhere(mine, other):
    positions = lax.axis_size("blk")
    chips, places = bits(lax.axis_size("grp"), positions)[1:], bits(positions, 1)
    x = mine + swap(other, "grp", 1)
    while chips or places:
        a, b = chips[:1], places[:1]
        chips, places = chips[1:], places[1:]
        if a and b:
            x = (x + swap(x, AXES, a[0])) + (swap(x, AXES, b[0]) + swap(x, AXES, a[0] | b[0]))
        else:
            x = x + swap(x, AXES, (a + b)[0])
    return x, swap(x, "grp", 1)


def per_device(tiles_near, near_cols, tiles_far, far_groups, need_blocks, start_vectors):
    tile = tiles_near.shape[1]
    blocks = start_vectors.shape[0] // tile
    sources = lax.axis_size("blk")
    groups = lax.axis_size("grp")
    shape = (blocks, sources, tiles_near.shape[0] // (blocks * sources), tile)
    total_rows = start_vectors.shape[0] * sources * groups
    place = jnp.stack([lax.axis_index("blk"), lax.axis_index("grp")]).astype(jnp.int32)
    scalars = (place, near_cols.reshape(-1), far_groups.reshape(-1))
    need = need_blocks.reshape(-1)
    wanted = swap(need_blocks, "grp", 1).reshape(-1)
    split = 3 * sources // 4

    def begin(rows):
        below = prepare(rows, need)
        far = [swap(below, "grp", k) for k in range(2, groups, 2)]
        near = near_rows(rows, rows)
        near[0] = (0, below)
        tiles = load(near[1][1], tiles_near, tiles_far)
        partial = near_product(shape, scalars, near[:split], tiles[0])
        tokens = [partial, *(x for _, x in near[split:])]
        far.append(swap(pack(tile, place, wanted, [below, *far], tokens), "grp", 1))
        partial = near_product(shape, scalars, near[split:], tiles[0], partial)
        return tiles, far, late(shape, scalars, need, partial, far, tiles[1])

    tiles, far, (product, rounded) = begin(start_vectors)
    past, copied = gram(tile, product, rounded)
    own, *outs = blocks_for_others(tile, place, rounded, far, past)
    near = near_rows(rounded, copied)
    far = [swap(x, "grp", 2 * i) for i, x in enumerate(outs, 1)]
    far.insert(0, swap(core_pack(own, far), "grp", 1))
    partial = early(shape, groups, scalars, near[:split], far, *tiles)
    moved, *halves = last(shape, scalars, partial, near[split:], tiles[0], past)
    vectors, low, scale, fine = finish(place, everywhere(*halves), moved, total_rows)

    def plain(start, vectors, low, scale):
        _, _, (product, _) = begin(start)
        current = scaled(product, scale, low, dot6).astype(BF16)
        _, _, (product, rounded) = begin(current)
        unit = jnp.eye(product.shape[1], dtype=F32) * start.shape[0]
        halves = everywhere(*halves_of(place, unit, gram(tile, product, rounded)[0]))
        return finish(place, halves, product, total_rows)[0]

    return lax.cond(fine[0] > 0, lambda start, vectors, low, scale: vectors, plain, start_vectors, vectors, low, scale)


def solution(mesh):
    in_specs = (
        P(AXES, None, None),
        P(AXES, None),
        P(AXES, None, None),
        P(AXES, None),
        P(AXES, None),
        P(AXES, None),
    )
    return jax.shard_map(
        per_device, mesh=mesh, in_specs=in_specs, out_specs=P(AXES, None), check_vma=False
    )
```

```python
import functools

import jax
import jax.numpy as jnp
from jax import lax
from jax.experimental import pallas as pl
from jax.experimental.pallas import tpu as pltpu
from jax.sharding import PartitionSpec as P

AXES = ("grp", "blk")
HIGHEST = lax.Precision.HIGHEST
INFLATION_MAX = 1.15
CORRECTION_MAX = 4e-6
VMEM = pl.BlockSpec(memory_space=pltpu.VMEM)
SMEM = pl.BlockSpec(memory_space=pltpu.SMEM)
ANY = pl.BlockSpec(memory_space=pl.ANY)
F32 = jnp.float32
NEED_ROWS = 16
DIAGONAL_ROWS = 8
BF16 = jnp.bfloat16
NN = (((1,), (0,)), ((), ()))
NT = (((1,), (1,)), ((), ()))
TN = (((0,), (0,)), ((), ()))


def cost(flops, nbytes):
    return pl.CostEstimate(flops=int(flops), bytes_accessed=int(nbytes), transcendentals=0)


def vmem(nbytes):
    return pltpu.CompilerParams(vmem_limit_bytes=int(nbytes) + (8 << 20))


def parts(x):
    high = x.astype(BF16)
    return high, (x - high.astype(F32)).astype(BF16)


def dot1(a, b, dims=NN):
    return lax.dot_general(a.astype(BF16), b.astype(BF16), dims, preferred_element_type=F32)


def dot3(a, b, dims=NN):
    a_high, a_low = parts(a)
    b_high, b_low = parts(b)
    (across,), (down,) = dims[0]
    return dot1(jnp.concatenate([a_high, a_low, a_high], across), jnp.concatenate([b_high, b_high, b_low], down), dims)


def dot6(a, b, dims=NN):
    return lax.dot_general(a, b, dims, precision=HIGHEST, preferred_element_type=F32)


def normalised(gram):
    _, on_diag = masks(gram.shape[0])
    diag = jnp.where(on_diag, gram, 0.0)
    scale_row = lax.rsqrt(jnp.sum(diag, axis=0, keepdims=True))
    scale_col = lax.rsqrt(jnp.sum(diag, axis=1, keepdims=True))
    return scale_row, gram * scale_col * scale_row - on_diag.astype(F32)


def iterated(base):
    below, on_diag = masks(base.shape[0])
    eye = on_diag.astype(F32)
    weight = below.astype(F32) + 0.5 * eye
    first = weight * base
    moved = dot1(first, base)
    low = first + weight * (dot1(moved, first, NT) - moved) + dot1(weight * moved, first)
    moved = dot3(low, base)
    crossed = dot3(low + moved - base, low, NT)
    step = weight * (base - low - moved + crossed - low * eye)
    return low + step - dot1(step, low), jnp.sum(step * step)


def eliminated(base, work):
    n = base.shape[0]
    rows = lax.broadcasted_iota(jnp.int32, (n, n), 0)
    cols = lax.broadcasted_iota(jnp.int32, (n, n), 1)
    eye = (rows == cols).astype(F32)
    work[0] = eye
    work[1] = base + eye

    def eliminate(j, carry):
        left = work[1]
        pivot_row = work[1, pl.ds(j, 1), :]
        pivot = jnp.sum(jnp.where(cols[:1] == j, pivot_row, 0.0), axis=1, keepdims=True)
        column = jnp.sum(jnp.where(cols == j, left, 0.0), axis=1, keepdims=True)
        factor = jnp.where(rows[:, :1] > j, column / pivot, 0.0)
        right_row = work[0, pl.ds(j, 1), :]
        work[1] = left - factor * pivot_row
        work[0] = work[0] - factor * right_row
        work[0, pl.ds(j, 1), :] = right_row * lax.rsqrt(pivot)
        return carry

    lax.fori_loop(0, n, eliminate, 0)
    return eye - work[0]


def masks(n):
    rows = lax.broadcasted_iota(jnp.int32, (n, n), 0)
    cols = lax.broadcasted_iota(jnp.int32, (n, n), 1)
    return rows > cols, rows == cols


def halved(place, a, b, whole, mine, other):
    n = whole.shape[0]
    half = n // 2
    below, diagonal = masks(n)
    whole[...] = jnp.where(jnp.logical_or(below, diagonal), b, a)
    row = jnp.sum(jnp.where(diagonal, a, 0.0), axis=0, keepdims=True)
    here = pl.multiple_of((place[1] & 1) * half, half)
    for ref, start in ((mine, here), (other, half - here)):
        ref[:half, :] = whole[pl.ds(start, half), :]
        ref[half:, :] = jnp.broadcast_to(row, (DIAGONAL_ROWS, n))


def unhalved(core, mine, other, whole):
    n = whole.shape[0]
    half = n // 2
    here = pl.multiple_of(core * half, half)
    whole[pl.ds(here, half), :] = mine[:half, :]
    whole[pl.ds(half - here, half), :] = other[:half, :]
    stored = whole[...]
    turned = stored.T
    below, diagonal = masks(n)
    a = jnp.where(diagonal, mine[half : half + 1, :], jnp.where(below, turned, stored))
    return a, jnp.where(jnp.logical_or(below, diagonal), stored, turned)


def scaled(x, scale, low, dot):
    x = x * scale
    return x - dot(x, low, NT)


def inflation_of(low):
    inverse = masks(low.shape[0])[1].astype(F32) - low
    return jnp.sum(inverse * inverse) / low.shape[0]


def both_factors(first, second, low_of, dot):
    _, on_diag = masks(first.shape[0])

    def as_column(row):
        return jnp.sum(jnp.where(on_diag, row, 0.0), axis=1, keepdims=True)

    scale, base = normalised(first)
    low = low_of(base)
    raw = second * scale * as_column(scale)
    raw = raw - dot(low, raw)
    raw = raw - dot(raw, low, NT)
    next_scale, base = normalised(raw)
    next_low = low_of(base)
    moved = as_column(next_scale) * low
    return low, scale, moved + next_low * next_scale - dot(next_low, moved), next_scale, next_low


def factors_kernel(total_rows, mine, other, low_ref, scale_ref, both_low_ref, both_scale_ref, fine_ref, whole, work):
    first, second = [x / total_rows for x in unhalved(lax.axis_index("grp") & 1, mine, other, whole)]
    sizes = []

    def quickly(base):
        low, size = iterated(base)
        sizes.append(size)
        return low

    *found, next_low = both_factors(first, second, quickly, dot3)
    refs = (low_ref, scale_ref, both_low_ref, both_scale_ref)
    for ref, value in zip(refs, found):
        ref[...] = value
    close = jnp.maximum(*sizes) <= CORRECTION_MAX
    fine = jnp.maximum(inflation_of(found[0]), inflation_of(next_low)) <= INFLATION_MAX
    fine_ref[0] = jnp.logical_and(close, fine).astype(jnp.int32)

    @pl.when(jnp.logical_not(close))
    def _():
        for ref, value in zip(refs, both_factors(first, second, lambda base: eliminated(base, work), dot6)):
            ref[...] = value


def factors(halves, total_rows):
    n = halves[0].shape[1]
    square, row = jax.ShapeDtypeStruct((n, n), F32), jax.ShapeDtypeStruct((1, n), F32)
    return pl.pallas_call(
        functools.partial(factors_kernel, total_rows),
        out_shape=(square, row, square, row, pltpu.SMEM((1,), jnp.int32)),
        in_specs=[VMEM] * 2,
        out_specs=(VMEM, VMEM, VMEM, VMEM, SMEM),
        scratch_shapes=[pltpu.VMEM((n, n), F32), pltpu.VMEM((2, n, n), F32)],
        cost_estimate=cost(60 * n**3, 8 * n * n),
        compiler_params=vmem(0),
        name="factors",
    )(*held(*halves))


def finish_kernel(dot, product, scale, low, next_scale, out_ref, done, sems):
    step = product.shape[0] // sems.shape[0]
    copies = []
    for i in range(sems.shape[0]):
        here = pl.ds(i * step, step)
        x = product[here, :] * scale[...]
        done[here, :] = x * next_scale[...] - dot(x, low[...], NT)
        copies.append(pltpu.make_async_copy(done.at[here, :], out_ref.at[here, :], sems.at[i]))
        copies[-1].start()
    for copy in copies:
        copy.wait()


def finish(dot, product, scale, low, next_scale):
    return pl.pallas_call(
        functools.partial(finish_kernel, dot),
        out_shape=pltpu.HBM(product.shape, F32),
        in_specs=[VMEM] * 4,
        out_specs=ANY,
        scratch_shapes=[pltpu.VMEM(product.shape, F32), pltpu.SemaphoreType.DMA((4,))],
        cost_estimate=cost(6 * product.size * product.shape[1], 8 * product.size),
        compiler_params=vmem(4 * product.size),
        name="finish",
    )(*held(product, scale, low, next_scale))


def entries(row):
    lane = lax.broadcasted_iota(jnp.int32, row.shape, 1)
    values = row[...]
    return lambda i: jnp.sum(jnp.where(lane == i, values, 0))


def add_near(shape, place, near_cols, tiles, near, r, acc):
    blocks, sources, per_source, tile = shape
    for k, ref in near:
        first = (r * sources + (place[0] ^ k)) * per_source
        for n in range(per_source):
            start = pl.multiple_of(near_cols(first + n) * tile, tile)
            part = jnp.dot(tiles[first + n], ref[pl.ds(start, tile), :], preferred_element_type=F32)
            acc = part if acc is None else acc + part
    return acc


def load_kernel(n, *refs):
    ins, outs, sems = refs[:n], refs[-n - 1 : -1], refs[-1]
    copies = [pltpu.make_async_copy(ins[i], outs[i], sems.at[i]) for i in range(n)]
    for copy in copies:
        copy.start()
    for copy in copies:
        copy.wait()


def load(token, *arrays):
    n = len(arrays)
    return pl.pallas_call(
        functools.partial(load_kernel, n),
        out_shape=tuple(pltpu.VMEM(a.shape, a.dtype) for a in arrays),
        in_specs=[ANY] * (n + 1),
        out_specs=(VMEM,) * n,
        scratch_shapes=[pltpu.SemaphoreType.DMA((n,))],
        cost_estimate=cost(0, sum(a.size * 4 for a in arrays)),
        compiler_params=vmem(0),
        name="load",
    )(*outside(*arrays), token)


def outside(*arrays):
    return [pltpu.with_memory_space_constraint(a, pltpu.HBM) for a in arrays]


def held(*arrays):
    return [pltpu.with_memory_space_constraint(a, pltpu.VMEM) for a in arrays]


def relay_kernel(x_ref, *refs):
    refs[-1][...] = x_ref[...]


def relay(x, *tokens):
    return pl.pallas_call(
        relay_kernel,
        out_shape=pltpu.VMEM(x.shape, x.dtype),
        in_specs=[VMEM] + [ANY] * len(tokens),
        out_specs=VMEM,
        cost_estimate=cost(0, 0),
        compiler_params=vmem(0),
        name="relay",
    )(*held(x), *tokens)


def prepare_kernel(rows, need, out_ref):
    n, width = rows.shape
    out_ref[:n, :] = rows[...]
    lanes = lax.broadcasted_iota(jnp.int32, (NEED_ROWS, width), 1)
    needs = jnp.zeros((NEED_ROWS, width), F32)
    for h in range(need.shape[0]):
        needs = jnp.where(lanes == h, need[h].astype(F32), needs)
    out_ref[n:, :] = needs.astype(BF16)


def prepare(rows, need):
    n, width = rows.shape
    return pl.pallas_call(
        prepare_kernel,
        out_shape=pltpu.VMEM((n + NEED_ROWS, width), BF16),
        in_specs=[VMEM, SMEM],
        out_specs=VMEM,
        cost_estimate=cost(0, 0),
        compiler_params=vmem(4 * rows.size),
        name="prepare",
    )(rows, need)


def pack_kernel(tile, n, wanted, *refs):
    out_ref = refs[-1]
    own = lax.axis_index("grp")
    lane = lax.broadcasted_iota(jnp.int32, wanted.shape, 1)
    needs = wanted[...]
    size = tile + NEED_ROWS
    for i, ref in enumerate(refs[:n]):
        block = jnp.sum(jnp.where(lane == (own ^ (2 * i)), needs, 0))
        start = pl.multiple_of(jnp.maximum(block, 0) * tile, tile)
        out_ref[i * size : i * size + tile, :] = ref[pl.ds(start, tile), :]
        out_ref[i * size + tile : (i + 1) * size, :] = ref[ref.shape[0] - NEED_ROWS :, :]


def pack(tile, wanted, rows, tokens):
    return pl.pallas_call(
        functools.partial(pack_kernel, tile, len(rows)),
        out_shape=pltpu.VMEM((len(rows) * (tile + NEED_ROWS), rows[0].shape[1]), BF16),
        in_specs=[VMEM] * (1 + len(rows)) + [ANY] * len(tokens),
        out_specs=VMEM,
        cost_estimate=cost(0, 0),
        compiler_params=vmem(0),
        name="pack",
    )(wanted, *held(*rows), *tokens)


def core_pack_kernel(tile, own, *refs):
    out_ref = refs[-1]
    out_ref[:tile, :] = own[...]
    for i, ref in enumerate(refs[:-1], 1):
        out_ref[i * tile : (i + 1) * tile, :] = ref[tile:, :]


def core_pack(own, received):
    tile, width = own.shape
    n = 1 + len(received)
    return pl.pallas_call(
        functools.partial(core_pack_kernel, tile),
        out_shape=pltpu.VMEM((n * tile, width), BF16),
        in_specs=[VMEM] * n,
        out_specs=VMEM,
        cost_estimate=cost(0, 0),
        compiler_params=vmem(0),
        name="core_pack",
    )(*held(own, *received))


def flat_rows(scalars):
    return [x.reshape(-1) for x in scalars]


def early_kernel(shape, distances, n_far, near_cols, far_groups, *refs):
    place = lax.axis_index("blk"), lax.axis_index("grp")
    near_cols, far_groups = near_cols.__getitem__, far_groups.__getitem__
    blocks, _, _, tile = shape
    n = len(distances)
    near = list(zip(distances, refs[:n]))
    packed, far = refs[n], refs[n + 1 : n + n_far]
    tiles_near, tiles_far, out_ref, table = refs[n + n_far :]
    for i in range(len(far) + 1):
        table[place[1] ^ (2 * i + 1)] = packed[i * tile : (i + 1) * tile, :]
        if i:
            table[place[1] ^ (2 * i)] = far[i - 1][:tile, :]
    for r in range(blocks):
        here = pl.ds(r * tile, tile)
        acc = add_near(shape, place, near_cols, tiles_near, near, r, None)
        out_ref[here, :] = add_far(far_groups, tiles_far, table, r, blocks, acc)


def early(shape, groups, scalars, near, far, tiles_near, tiles_far):
    blocks, _, _, tile = shape
    distances, rows = zip(*near)
    width = rows[0].shape[1]
    return pl.pallas_call(
        functools.partial(early_kernel, shape, distances, len(far)),
        out_shape=pltpu.VMEM((blocks * tile, width), F32),
        in_specs=[SMEM] * 2 + [VMEM] * (len(rows) + len(far) + 2),
        out_specs=VMEM,
        scratch_shapes=[pltpu.VMEM((groups, tile, width), BF16)],
        cost_estimate=cost(0, 0),
        compiler_params=vmem(0),
        name="early",
    )(*flat_rows(scalars), *held(*rows, *far, tiles_near, tiles_far))


def near_kernel(shape, distances, near_cols, *refs):
    place = lax.axis_index("blk"), lax.axis_index("grp")
    near_cols = near_cols.__getitem__
    blocks, _, _, tile = shape
    n = len(distances)
    *before, tiles, out_ref = refs[n:]
    near = list(zip(distances, refs[:n]))
    for r in range(blocks):
        here = pl.ds(r * tile, tile)
        acc = before[0][here, :] if before else None
        out_ref[here, :] = add_near(shape, place, near_cols, tiles, near, r, acc)


def near_product(shape, scalars, near, tiles, *before):
    blocks, _, _, tile = shape
    distances, rows = zip(*near)
    return pl.pallas_call(
        functools.partial(near_kernel, shape, distances),
        out_shape=pltpu.VMEM((blocks * tile, rows[0].shape[1]), F32),
        in_specs=[SMEM] + [VMEM] * (len(rows) + len(before) + 1),
        out_specs=VMEM,
        cost_estimate=cost(0, 0),
        compiler_params=vmem(0),
        name="near",
    )(*flat_rows(scalars[:1]), *held(*rows, *before, tiles))


def far_table(place, need, far, packed, table):
    tile = table.shape[1]
    size = tile + NEED_ROWS
    for i in range(len(far) + 1):
        h = place[1] ^ (2 * i)
        table[h ^ 1] = packed[i * size : i * size + tile, :]
        if i:
            start = pl.multiple_of(jnp.maximum(need(h), 0) * tile, tile)
            table[h] = far[i - 1][pl.ds(start, tile), :]


def add_far(far_groups, tiles, table, r, blocks, acc):
    each = tiles.shape[0] // blocks
    for t in range(r * each, (r + 1) * each):
        acc = acc + jnp.dot(tiles[t], table[far_groups(t)], preferred_element_type=F32)
    return acc


def gram_of(rows, tile):
    gram = None
    for start in range(0, rows.shape[0], tile):
        both = jnp.concatenate(parts(rows[pl.ds(start, tile), :]), axis=1)
        part = lax.dot_general(both, both, TN, preferred_element_type=F32)
        gram = part if gram is None else gram + part
    n = rows.shape[1]
    crossed = gram[:n, n:]
    return gram[:n, :n] + (crossed + crossed.T) + gram[n:, n:]


def late_kernel(shape, far_groups, need, partial, *refs):
    place = lax.axis_index("blk"), lax.axis_index("grp")
    groups = need.shape[1]
    far_groups, need = entries(far_groups), entries(need)
    blocks, _, _, tile = shape
    *far, packed, tiles = refs[: groups // 2 + 1]
    product_ref, rounded_ref, table = refs[groups // 2 + 1 :]
    far_table(place, need, far, packed, table)
    for r in range(blocks):
        here = pl.ds(r * tile, tile)
        acc = add_far(far_groups, tiles, table, r, blocks, partial[here, :])
        product_ref[here, :] = acc
        rounded_ref[here, :] = acc.astype(BF16)


def late(shape, scalars, need, partial, far, tiles):
    n, width = partial.shape
    groups, tile = need.shape[1], shape[3]
    return pl.pallas_call(
        functools.partial(late_kernel, shape),
        out_shape=(pltpu.VMEM((n, width), F32), pltpu.VMEM((n, width), BF16)),
        in_specs=[VMEM] * (len(far) + 4),
        out_specs=(VMEM,) * 2,
        scratch_shapes=[pltpu.VMEM((groups, tile, width), BF16)],
        cost_estimate=cost(0, 0),
        compiler_params=vmem(0),
        name="late",
    )(scalars[1], need, *held(partial, *far, tiles))


def gram_kernel(tile, product, rounded, out_ref, copy_ref):
    out_ref[...] = gram_of(product, tile)
    copy_ref[...] = rounded[...]


def gram(tile, product, rounded):
    width = product.shape[1]
    return pl.pallas_call(
        functools.partial(gram_kernel, tile),
        out_shape=(pltpu.VMEM((width, width), F32), pltpu.VMEM(rounded.shape, BF16)),
        in_specs=[VMEM] * 2,
        out_specs=(VMEM,) * 2,
        cost_estimate=cost(0, 0),
        compiler_params=vmem(0),
        name="gram",
    )(*held(product, rounded))


def halves_kernel(a, b, mine, other, whole):
    place = lax.axis_index("blk"), lax.axis_index("grp")
    halved(place, a[...], b[...], whole, mine, other)


def halves_of(a, b):
    n = a.shape[0]
    half = pltpu.VMEM((n // 2 + DIAGONAL_ROWS, n), F32)
    return pl.pallas_call(
        halves_kernel,
        out_shape=(half, half),
        in_specs=[VMEM] * 2,
        out_specs=(VMEM,) * 2,
        scratch_shapes=[pltpu.VMEM((n, n), F32)],
        compiler_params=vmem(0),
        name="halves",
    )(a, b)


def blocks_kernel(tile, n_far, rounded, *refs):
    place = lax.axis_index("blk"), lax.axis_index("grp")
    *far, packed = refs[:n_far]
    own_ref, *outs = refs[n_far + 1 :]
    lane = lax.broadcasted_iota(jnp.int32, (1, rounded.shape[1]), 1) == place[1]
    size = tile + NEED_ROWS

    def wanted_block(k):
        ref, first = (packed, k // 2 * size + tile) if k % 2 else (far[k // 2 - 1], far[0].shape[0] - NEED_ROWS)
        needs = ref[first : first + NEED_ROWS, :].astype(F32)[:1]
        block = jnp.maximum(jnp.sum(jnp.where(lane, needs, 0.0)).astype(jnp.int32), 0)
        return rounded[pl.ds(pl.multiple_of(block * tile, tile), tile), :]

    own_ref[...] = wanted_block(1)
    for i, out_ref in enumerate(outs, 1):
        out_ref[:tile, :] = wanted_block(2 * i)
        out_ref[tile:, :] = wanted_block(2 * i + 1)


def blocks_for_others(tile, rounded, far, token):
    width = rounded.shape[1]
    pair = pltpu.VMEM((2 * tile, width), BF16)
    return pl.pallas_call(
        functools.partial(blocks_kernel, tile, len(far)),
        out_shape=(pltpu.VMEM((tile, width), BF16), *(pair,) * (len(far) - 1)),
        in_specs=[VMEM] * (1 + len(far)) + [ANY],
        out_specs=(VMEM,) * len(far),
        cost_estimate=cost(0, 0),
        compiler_params=vmem(0),
        name="blocks",
    )(*held(rounded, *far), token)


def last_kernel(shape, distances, near_cols, partial, *refs):
    place = lax.axis_index("blk"), lax.axis_index("grp")
    near_cols = entries(near_cols)
    blocks, _, _, tile = shape
    n = len(distances)
    near = list(zip(distances, refs[:n]))
    past, tiles, product_ref, mine, other, whole = refs[n:]
    for r in range(blocks):
        here = pl.ds(r * tile, tile)
        product_ref[here, :] = add_near(shape, place, near_cols, tiles, near, r, partial[here, :])
    halved(place, past[...], gram_of(product_ref, tile), whole, mine, other)


def last(shape, scalars, partial, near, tiles, past):
    distances, rows = zip(*near)
    width = partial.shape[1]
    half = pltpu.VMEM((width // 2 + DIAGONAL_ROWS, width), F32)
    return pl.pallas_call(
        functools.partial(last_kernel, shape, distances),
        out_shape=(pltpu.VMEM(partial.shape, F32), half, half),
        in_specs=[VMEM] * (len(rows) + 4),
        out_specs=(VMEM,) * 3,
        scratch_shapes=[pltpu.VMEM((width, width), F32)],
        cost_estimate=cost(0, 0),
        compiler_params=vmem(0),
        name="last",
    )(scalars[0], *held(partial, *rows, past, tiles))


def swap(x, axis, mask):
    size = lax.axis_size(axis)
    return lax.ppermute(x, axis, [(i, i ^ mask) for i in range(size)])


def near_rows(rows, again):
    step = lax.axis_size("blk") // 2
    here = [(0, rows), (step, swap(rows, "blk", step))]
    while step > 1:
        step //= 2
        direct = swap(again, "blk", step)
        here += [(step, direct)] + [(k | step, swap(relay(x, direct), "blk", step)) for k, x in here[1:]]
    return here


def bits(size, scale):
    return [scale << i for i in range(size.bit_length() - 1)]


def everywhere(mine, other):
    positions = lax.axis_size("blk")
    chips, places = bits(lax.axis_size("grp"), positions)[1:], bits(positions, 1)
    x = mine + swap(other, "grp", 1)
    while chips or places:
        a, b = chips[:1], places[:1]
        chips, places = chips[1:], places[1:]
        if a and b:
            x = (x + swap(x, AXES, a[0])) + (swap(x, AXES, b[0]) + swap(x, AXES, a[0] | b[0]))
        else:
            x = x + swap(x, AXES, (a + b)[0])
    return x, swap(x, "grp", 1)


def per_device(tiles_near, near_cols, tiles_far, far_groups, need_blocks, start_vectors):
    tile = tiles_near.shape[1]
    blocks = start_vectors.shape[0] // tile
    sources = lax.axis_size("blk")
    groups = lax.axis_size("grp")
    shape = (blocks, sources, tiles_near.shape[0] // (blocks * sources), tile)
    total_rows = start_vectors.shape[0] * sources * groups
    scalars = (near_cols, far_groups)
    wanted = swap(need_blocks, "grp", 1)
    split = 3 * sources // 4

    def begin(rows):
        below = prepare(rows, need_blocks.reshape(-1))
        far = [swap(below, "grp", k) for k in range(2, groups, 2)]
        near = near_rows(rows, rows)
        near[0] = (0, below)
        tiles = load(near[1][1], tiles_near, tiles_far)
        partial = near_product(shape, scalars, near[:split], tiles[0])
        tokens = [partial, *(x for _, x in near[split:])]
        far.append(swap(pack(tile, wanted, [below, *far], tokens), "grp", 1))
        partial = near_product(shape, scalars, near[split:], tiles[0], partial)
        return tiles, far, late(shape, scalars, need_blocks, partial, far, tiles[1])

    tiles, far, (product, rounded) = begin(start_vectors)
    past, copied = gram(tile, product, rounded)
    own, *outs = blocks_for_others(tile, rounded, far, past)
    near = near_rows(rounded, copied)
    far = [swap(x, "grp", 2 * i) for i, x in enumerate(outs, 1)]
    far.insert(0, swap(core_pack(own, far), "grp", 1))
    partial = early(shape, groups, scalars, near[:split], far, *tiles)
    moved, *halves = last(shape, scalars, partial, near[split:], tiles[0], past)
    low, scale, both_low, next_scale, fine = factors(everywhere(*halves), total_rows)
    vectors = finish(dot3, moved, scale, both_low, next_scale)

    def plain(start, vectors, low, scale):
        _, _, (product, _) = begin(start)
        current = scaled(product, scale, low, dot6).astype(BF16)
        _, _, (product, rounded) = begin(current)
        unit = jnp.eye(product.shape[1], dtype=F32) * start.shape[0]
        halves = everywhere(*halves_of(unit, gram(tile, product, rounded)[0]))
        _, scale, both_low, next_scale, _ = factors(halves, total_rows)
        return finish(dot6, product, scale, both_low, next_scale)

    branches = [plain, lambda start, vectors, low, scale: vectors]
    return lax.switch(fine[0], branches, start_vectors, vectors, low, scale)


def solution(mesh):
    in_specs = (
        P(AXES, None, None),
        P(AXES, None),
        P(AXES, None, None),
        P(AXES, None),
        P(AXES, None),
        P(AXES, None),
    )
    return jax.shard_map(
        per_device, mesh=mesh, in_specs=in_specs, out_specs=P(AXES, None), check_vma=False
    )
```

```python
import functools

import jax
import jax.numpy as jnp
from jax import lax
from jax.experimental import pallas as pl
from jax.experimental.pallas import tpu as pltpu
from jax.sharding import PartitionSpec as P

AXES = ("grp", "blk")
HIGHEST = lax.Precision.HIGHEST
INFLATION_MAX = 1.15
CORRECTION_MAX = 4e-6
VMEM = pl.BlockSpec(memory_space=pltpu.VMEM)
SMEM = pl.BlockSpec(memory_space=pltpu.SMEM)
ANY = pl.BlockSpec(memory_space=pl.ANY)
F32 = jnp.float32
NEED_ROWS = 16
DIAGONAL_ROWS = 8
BF16 = jnp.bfloat16
NN = (((1,), (0,)), ((), ()))
NT = (((1,), (1,)), ((), ()))
TN = (((0,), (0,)), ((), ()))


def cost(flops, nbytes):
    return pl.CostEstimate(flops=int(flops), bytes_accessed=int(nbytes), transcendentals=0)


def vmem(nbytes):
    return pltpu.CompilerParams(vmem_limit_bytes=int(nbytes) + (8 << 20))


def parts(x):
    high = x.astype(BF16)
    return high, (x - high.astype(F32)).astype(BF16)


def dot1(a, b, dims=NN):
    return lax.dot_general(a.astype(BF16), b.astype(BF16), dims, preferred_element_type=F32)


def dot3(a, b, dims=NN):
    a_high, a_low = parts(a)
    b_high, b_low = parts(b)
    (across,), (down,) = dims[0]
    return dot1(jnp.concatenate([a_high, a_low, a_high], across), jnp.concatenate([b_high, b_high, b_low], down), dims)


def dot6(a, b, dims=NN):
    return lax.dot_general(a, b, dims, precision=HIGHEST, preferred_element_type=F32)


def normalised(gram):
    _, on_diag = masks(gram.shape[0])
    diag = jnp.where(on_diag, gram, 0.0)
    scale_row = lax.rsqrt(jnp.sum(diag, axis=0, keepdims=True))
    scale_col = lax.rsqrt(jnp.sum(diag, axis=1, keepdims=True))
    return scale_row, gram * scale_col * scale_row - on_diag.astype(F32)


def iterated(base):
    below, on_diag = masks(base.shape[0])
    eye = on_diag.astype(F32)
    weight = below.astype(F32) + 0.5 * eye
    first = weight * base
    moved = dot1(first, base)
    low = first + weight * (dot1(moved, first, NT) - moved) + dot1(weight * moved, first)
    moved = dot3(low, base)
    crossed = dot3(low + moved - base, low, NT)
    step = weight * (base - low - moved + crossed - low * eye)
    return low + step - dot1(step, low), jnp.sum(step * step)


def eliminated(base, work):
    n = base.shape[0]
    rows = lax.broadcasted_iota(jnp.int32, (n, n), 0)
    cols = lax.broadcasted_iota(jnp.int32, (n, n), 1)
    eye = (rows == cols).astype(F32)
    work[0] = eye
    work[1] = base + eye

    def eliminate(j, carry):
        left = work[1]
        pivot_row = work[1, pl.ds(j, 1), :]
        pivot = jnp.sum(jnp.where(cols[:1] == j, pivot_row, 0.0), axis=1, keepdims=True)
        column = jnp.sum(jnp.where(cols == j, left, 0.0), axis=1, keepdims=True)
        factor = jnp.where(rows[:, :1] > j, column / pivot, 0.0)
        right_row = work[0, pl.ds(j, 1), :]
        work[1] = left - factor * pivot_row
        work[0] = work[0] - factor * right_row
        work[0, pl.ds(j, 1), :] = right_row * lax.rsqrt(pivot)
        return carry

    lax.fori_loop(0, n, eliminate, 0)
    return eye - work[0]


def masks(n):
    rows = lax.broadcasted_iota(jnp.int32, (n, n), 0)
    cols = lax.broadcasted_iota(jnp.int32, (n, n), 1)
    return rows > cols, rows == cols


def halved(place, a, b, whole, mine, other):
    n = whole.shape[0]
    half = n // 2
    below, diagonal = masks(n)
    whole[...] = jnp.where(jnp.logical_or(below, diagonal), b, a)
    row = jnp.sum(jnp.where(diagonal, a, 0.0), axis=0, keepdims=True)
    here = pl.multiple_of((place[1] & 1) * half, half)
    for ref, start in ((mine, here), (other, half - here)):
        ref[:half, :] = whole[pl.ds(start, half), :]
        ref[half:, :] = jnp.broadcast_to(row, (DIAGONAL_ROWS, n))


def unhalved(core, mine, other, whole):
    n = whole.shape[0]
    half = n // 2
    here = pl.multiple_of(core * half, half)
    whole[pl.ds(here, half), :] = mine[:half, :]
    whole[pl.ds(half - here, half), :] = other[:half, :]
    stored = whole[...]
    turned = stored.T
    below, diagonal = masks(n)
    a = jnp.where(diagonal, mine[half : half + 1, :], jnp.where(below, turned, stored))
    return a, jnp.where(jnp.logical_or(below, diagonal), stored, turned)


def scaled(x, scale, low, dot):
    x = x * scale
    return x - dot(x, low, NT)


def inflation_of(low):
    inverse = masks(low.shape[0])[1].astype(F32) - low
    return jnp.sum(inverse * inverse) / low.shape[0]


def both_factors(first, second, low_of, dot):
    _, on_diag = masks(first.shape[0])

    def as_column(row):
        return jnp.sum(jnp.where(on_diag, row, 0.0), axis=1, keepdims=True)

    scale, base = normalised(first)
    low = low_of(base)
    raw = second * scale * as_column(scale)
    raw = raw - dot(low, raw)
    raw = raw - dot(raw, low, NT)
    next_scale, base = normalised(raw)
    next_low = low_of(base)
    moved = as_column(next_scale) * low
    return low, scale, moved + next_low * next_scale - dot(next_low, moved), next_scale, next_low


def factors_kernel(total_rows, mine, other, low_ref, scale_ref, both_low_ref, both_scale_ref, fine_ref, whole, work):
    first, second = [x / total_rows for x in unhalved(lax.axis_index("grp") & 1, mine, other, whole)]
    sizes = []

    def quickly(base):
        low, size = iterated(base)
        sizes.append(size)
        return low

    *found, next_low = both_factors(first, second, quickly, dot3)
    refs = (low_ref, scale_ref, both_low_ref, both_scale_ref)
    for ref, value in zip(refs, found):
        ref[...] = value
    close = jnp.maximum(*sizes) <= CORRECTION_MAX
    fine = jnp.maximum(inflation_of(found[0]), inflation_of(next_low)) <= INFLATION_MAX
    fine_ref[0] = jnp.logical_and(close, fine).astype(jnp.int32)

    @pl.when(jnp.logical_not(close))
    def _():
        for ref, value in zip(refs, both_factors(first, second, lambda base: eliminated(base, work), dot6)):
            ref[...] = value


def factors(halves, total_rows):
    n = halves[0].shape[1]
    square, row = jax.ShapeDtypeStruct((n, n), F32), jax.ShapeDtypeStruct((1, n), F32)
    return pl.pallas_call(
        functools.partial(factors_kernel, total_rows),
        out_shape=(square, row, square, row, pltpu.SMEM((1,), jnp.int32)),
        in_specs=[VMEM] * 2,
        out_specs=(VMEM, VMEM, VMEM, VMEM, SMEM),
        scratch_shapes=[pltpu.VMEM((n, n), F32), pltpu.VMEM((2, n, n), F32)],
        cost_estimate=cost(60 * n**3, 8 * n * n),
        compiler_params=vmem(0),
        name="factors",
    )(*held(*halves))


def finish_kernel(dot, product, scale, low, next_scale, out_ref, done, sems):
    step = product.shape[0] // sems.shape[0]
    copies = []
    for i in range(sems.shape[0]):
        here = pl.ds(i * step, step)
        x = product[here, :] * scale[...]
        done[here, :] = x * next_scale[...] - dot(x, low[...], NT)
        copies.append(pltpu.make_async_copy(done.at[here, :], out_ref.at[here, :], sems.at[i]))
        copies[-1].start()
    for copy in copies:
        copy.wait()


def finish(dot, product, scale, low, next_scale):
    return pl.pallas_call(
        functools.partial(finish_kernel, dot),
        out_shape=pltpu.HBM(product.shape, F32),
        in_specs=[VMEM] * 4,
        out_specs=ANY,
        scratch_shapes=[pltpu.VMEM(product.shape, F32), pltpu.SemaphoreType.DMA((4,))],
        cost_estimate=cost(6 * product.size * product.shape[1], 8 * product.size),
        compiler_params=vmem(4 * product.size),
        name="finish",
    )(*held(product, scale, low, next_scale))


def entries(row):
    lane = lax.broadcasted_iota(jnp.int32, row.shape, 1)
    values = row[...]
    return lambda i: jnp.sum(jnp.where(lane == i, values, 0))


def add_near(shape, place, near_cols, tiles, near, r, acc):
    blocks, sources, per_source, tile = shape
    for k, ref in near:
        first = (r * sources + (place[0] ^ k)) * per_source
        for n in range(per_source):
            start = pl.multiple_of(near_cols(first + n) * tile, tile)
            part = jnp.dot(tiles[first + n], ref[pl.ds(start, tile), :], preferred_element_type=F32)
            acc = part if acc is None else acc + part
    return acc


def load_kernel(n, *refs):
    ins, outs, sems = refs[:n], refs[-n - 1 : -1], refs[-1]
    copies = [pltpu.make_async_copy(ins[i], outs[i], sems.at[i]) for i in range(n)]
    for copy in copies:
        copy.start()
    for copy in copies:
        copy.wait()


def load(token, *arrays):
    n = len(arrays)
    return pl.pallas_call(
        functools.partial(load_kernel, n),
        out_shape=tuple(pltpu.VMEM(a.shape, a.dtype) for a in arrays),
        in_specs=[ANY] * (n + 1),
        out_specs=(VMEM,) * n,
        scratch_shapes=[pltpu.SemaphoreType.DMA((n,))],
        cost_estimate=cost(0, sum(a.size * 4 for a in arrays)),
        compiler_params=vmem(0),
        name="load",
    )(*outside(*arrays), token)


def outside(*arrays):
    return [pltpu.with_memory_space_constraint(a, pltpu.HBM) for a in arrays]


def held(*arrays):
    return [pltpu.with_memory_space_constraint(a, pltpu.VMEM) for a in arrays]


def relay_kernel(x_ref, *refs):
    refs[-1][...] = x_ref[...]


def relay(x, *tokens):
    return pl.pallas_call(
        relay_kernel,
        out_shape=pltpu.VMEM(x.shape, x.dtype),
        in_specs=[VMEM] + [ANY] * len(tokens),
        out_specs=VMEM,
        cost_estimate=cost(0, 0),
        compiler_params=vmem(0),
        name="relay",
    )(*held(x), *tokens)


def prepare_kernel(rows, need, out_ref):
    n, width = rows.shape
    out_ref[:n, :] = rows[...]
    lanes = lax.broadcasted_iota(jnp.int32, (NEED_ROWS, width), 1)
    needs = jnp.zeros((NEED_ROWS, width), F32)
    for h in range(need.shape[0]):
        needs = jnp.where(lanes == h, need[h].astype(F32), needs)
    out_ref[n:, :] = needs.astype(BF16)


def prepare(rows, need):
    n, width = rows.shape
    return pl.pallas_call(
        prepare_kernel,
        out_shape=pltpu.VMEM((n + NEED_ROWS, width), BF16),
        in_specs=[VMEM, SMEM],
        out_specs=VMEM,
        cost_estimate=cost(0, 0),
        compiler_params=vmem(4 * rows.size),
        name="prepare",
    )(rows, need)


def pack_kernel(tile, n, wanted, *refs):
    out_ref = refs[-1]
    own = lax.axis_index("grp")
    lane = lax.broadcasted_iota(jnp.int32, wanted.shape, 1)
    needs = wanted[...]
    size = tile + NEED_ROWS
    for i, ref in enumerate(refs[:n]):
        block = jnp.sum(jnp.where(lane == (own ^ (2 * i)), needs, 0))
        start = pl.multiple_of(jnp.maximum(block, 0) * tile, tile)
        out_ref[i * size : i * size + tile, :] = ref[pl.ds(start, tile), :]
        out_ref[i * size + tile : (i + 1) * size, :] = ref[ref.shape[0] - NEED_ROWS :, :]


def pack(tile, wanted, rows, tokens):
    return pl.pallas_call(
        functools.partial(pack_kernel, tile, len(rows)),
        out_shape=pltpu.VMEM((len(rows) * (tile + NEED_ROWS), rows[0].shape[1]), BF16),
        in_specs=[VMEM] * (1 + len(rows)) + [ANY] * len(tokens),
        out_specs=VMEM,
        cost_estimate=cost(0, 0),
        compiler_params=vmem(0),
        name="pack",
    )(wanted, *held(*rows), *tokens)


def core_pack_kernel(tile, n, own, *refs):
    out_ref = refs[-1]
    out_ref[:tile, :] = own[...]
    for i, ref in enumerate(refs[:n], 1):
        out_ref[i * tile : (i + 1) * tile, :] = ref[tile:, :]


def core_pack(own, received, token):
    tile, width = own.shape
    n = 1 + len(received)
    return pl.pallas_call(
        functools.partial(core_pack_kernel, tile, n - 1),
        out_shape=pltpu.VMEM((n * tile, width), BF16),
        in_specs=[VMEM] * n + [ANY],
        out_specs=VMEM,
        cost_estimate=cost(0, 0),
        compiler_params=vmem(0),
        name="core_pack",
    )(*held(own, *received), token)


def flat_rows(scalars):
    return [x.reshape(-1) for x in scalars]


def early_kernel(shape, distances, n_far, near_cols, far_groups, *refs):
    place = lax.axis_index("blk"), lax.axis_index("grp")
    near_cols, far_groups = near_cols.__getitem__, far_groups.__getitem__
    blocks, _, _, tile = shape
    n = len(distances)
    near = list(zip(distances, refs[:n]))
    packed, far = refs[n], refs[n + 1 : n + n_far]
    tiles_near, tiles_far, out_ref, table = refs[n + n_far :]
    for i in range(len(far) + 1):
        table[place[1] ^ (2 * i + 1)] = packed[i * tile : (i + 1) * tile, :]
        if i:
            table[place[1] ^ (2 * i)] = far[i - 1][:tile, :]
    for r in range(blocks):
        here = pl.ds(r * tile, tile)
        acc = add_near(shape, place, near_cols, tiles_near, near, r, None)
        out_ref[here, :] = add_far(far_groups, tiles_far, table, r, blocks, acc)


def early(shape, groups, scalars, near, far, tiles_near, tiles_far):
    blocks, _, _, tile = shape
    distances, rows = zip(*near)
    width = rows[0].shape[1]
    return pl.pallas_call(
        functools.partial(early_kernel, shape, distances, len(far)),
        out_shape=pltpu.VMEM((blocks * tile, width), F32),
        in_specs=[SMEM] * 2 + [VMEM] * (len(rows) + len(far) + 2),
        out_specs=VMEM,
        scratch_shapes=[pltpu.VMEM((groups, tile, width), BF16)],
        cost_estimate=cost(0, 0),
        compiler_params=vmem(0),
        name="early",
    )(*flat_rows(scalars), *held(*rows, *far, tiles_near, tiles_far))


def near_kernel(shape, distances, near_cols, *refs):
    place = lax.axis_index("blk"), lax.axis_index("grp")
    near_cols = near_cols.__getitem__
    blocks, _, _, tile = shape
    n = len(distances)
    *before, tiles, out_ref = refs[n:]
    near = list(zip(distances, refs[:n]))
    for r in range(blocks):
        here = pl.ds(r * tile, tile)
        acc = before[0][here, :] if before else None
        out_ref[here, :] = add_near(shape, place, near_cols, tiles, near, r, acc)


def near_product(shape, scalars, near, tiles, *before):
    blocks, _, _, tile = shape
    distances, rows = zip(*near)
    return pl.pallas_call(
        functools.partial(near_kernel, shape, distances),
        out_shape=pltpu.VMEM((blocks * tile, rows[0].shape[1]), F32),
        in_specs=[SMEM] + [VMEM] * (len(rows) + len(before) + 1),
        out_specs=VMEM,
        cost_estimate=cost(0, 0),
        compiler_params=vmem(0),
        name="near",
    )(*flat_rows(scalars[:1]), *held(*rows, *before, tiles))


def far_table(place, need, far, packed, table):
    tile = table.shape[1]
    size = tile + NEED_ROWS
    for i in range(len(far) + 1):
        h = place[1] ^ (2 * i)
        table[h ^ 1] = packed[i * size : i * size + tile, :]
        if i:
            start = pl.multiple_of(jnp.maximum(need(h), 0) * tile, tile)
            table[h] = far[i - 1][pl.ds(start, tile), :]


def add_far(far_groups, tiles, table, r, blocks, acc):
    each = tiles.shape[0] // blocks
    for t in range(r * each, (r + 1) * each):
        acc = acc + jnp.dot(tiles[t], table[far_groups(t)], preferred_element_type=F32)
    return acc


def gram_of(rows, tile):
    gram = None
    for start in range(0, rows.shape[0], tile):
        both = jnp.concatenate(parts(rows[pl.ds(start, tile), :]), axis=1)
        part = lax.dot_general(both, both, TN, preferred_element_type=F32)
        gram = part if gram is None else gram + part
    n = rows.shape[1]
    crossed = gram[:n, n:]
    return gram[:n, :n] + (crossed + crossed.T) + gram[n:, n:]


def late_kernel(shape, far_groups, need, partial, *refs):
    place = lax.axis_index("blk"), lax.axis_index("grp")
    groups = need.shape[1]
    far_groups, need = entries(far_groups), entries(need)
    blocks, _, _, tile = shape
    *far, packed, tiles = refs[: groups // 2 + 1]
    product_ref, rounded_ref, table = refs[groups // 2 + 1 :]
    far_table(place, need, far, packed, table)
    for r in range(blocks):
        here = pl.ds(r * tile, tile)
        acc = add_far(far_groups, tiles, table, r, blocks, partial[here, :])
        product_ref[here, :] = acc
        rounded_ref[here, :] = acc.astype(BF16)


def late(shape, scalars, need, partial, far, tiles):
    n, width = partial.shape
    groups, tile = need.shape[1], shape[3]
    return pl.pallas_call(
        functools.partial(late_kernel, shape),
        out_shape=(pltpu.VMEM((n, width), F32), pltpu.VMEM((n, width), BF16)),
        in_specs=[VMEM] * (len(far) + 4),
        out_specs=(VMEM,) * 2,
        scratch_shapes=[pltpu.VMEM((groups, tile, width), BF16)],
        cost_estimate=cost(0, 0),
        compiler_params=vmem(0),
        name="late",
    )(scalars[1], need, *held(partial, *far, tiles))


def gram_kernel(tile, product, out_ref):
    out_ref[...] = gram_of(product, tile)


def gram(tile, product):
    width = product.shape[1]
    return pl.pallas_call(
        functools.partial(gram_kernel, tile),
        out_shape=pltpu.VMEM((width, width), F32),
        in_specs=[VMEM],
        out_specs=VMEM,
        cost_estimate=cost(0, 0),
        compiler_params=vmem(0),
        name="gram",
    )(*held(product))


def halves_kernel(a, b, mine, other, whole):
    place = lax.axis_index("blk"), lax.axis_index("grp")
    halved(place, a[...], b[...], whole, mine, other)


def halves_of(a, b):
    n = a.shape[0]
    half = pltpu.VMEM((n // 2 + DIAGONAL_ROWS, n), F32)
    return pl.pallas_call(
        halves_kernel,
        out_shape=(half, half),
        in_specs=[VMEM] * 2,
        out_specs=(VMEM,) * 2,
        scratch_shapes=[pltpu.VMEM((n, n), F32)],
        compiler_params=vmem(0),
        name="halves",
    )(a, b)


def blocks_kernel(tile, n_far, rounded, *refs):
    place = lax.axis_index("blk"), lax.axis_index("grp")
    *far, packed = refs[:n_far]
    own_ref, *outs = refs[n_far + 1 :]
    lane = lax.broadcasted_iota(jnp.int32, (1, rounded.shape[1]), 1) == place[1]
    size = tile + NEED_ROWS

    def wanted_block(k):
        ref, first = (packed, k // 2 * size + tile) if k % 2 else (far[k // 2 - 1], far[0].shape[0] - NEED_ROWS)
        needs = ref[first : first + NEED_ROWS, :].astype(F32)[:1]
        block = jnp.maximum(jnp.sum(jnp.where(lane, needs, 0.0)).astype(jnp.int32), 0)
        return rounded[pl.ds(pl.multiple_of(block * tile, tile), tile), :]

    own_ref[...] = wanted_block(1)
    for i, out_ref in enumerate(outs, 1):
        out_ref[:tile, :] = wanted_block(2 * i)
        out_ref[tile:, :] = wanted_block(2 * i + 1)


def blocks_for_others(tile, rounded, far, token):
    width = rounded.shape[1]
    pair = pltpu.VMEM((2 * tile, width), BF16)
    return pl.pallas_call(
        functools.partial(blocks_kernel, tile, len(far)),
        out_shape=(pltpu.VMEM((tile, width), BF16), *(pair,) * (len(far) - 1)),
        in_specs=[VMEM] * (1 + len(far)) + [ANY],
        out_specs=(VMEM,) * len(far),
        cost_estimate=cost(0, 0),
        compiler_params=vmem(0),
        name="blocks",
    )(*held(rounded, *far), token)


def last_kernel(shape, distances, near_cols, partial, *refs):
    place = lax.axis_index("blk"), lax.axis_index("grp")
    near_cols = entries(near_cols)
    blocks, _, _, tile = shape
    n = len(distances)
    near = list(zip(distances, refs[:n]))
    past, tiles, product_ref, mine, other, whole = refs[n:]
    for r in range(blocks):
        here = pl.ds(r * tile, tile)
        product_ref[here, :] = add_near(shape, place, near_cols, tiles, near, r, partial[here, :])
    halved(place, past[...], gram_of(product_ref, tile), whole, mine, other)


def last(shape, scalars, partial, near, tiles, past):
    distances, rows = zip(*near)
    width = partial.shape[1]
    half = pltpu.VMEM((width // 2 + DIAGONAL_ROWS, width), F32)
    return pl.pallas_call(
        functools.partial(last_kernel, shape, distances),
        out_shape=(pltpu.VMEM(partial.shape, F32), half, half),
        in_specs=[VMEM] * (len(rows) + 4),
        out_specs=(VMEM,) * 3,
        scratch_shapes=[pltpu.VMEM((width, width), F32)],
        cost_estimate=cost(0, 0),
        compiler_params=vmem(0),
        name="last",
    )(scalars[0], *held(partial, *rows, past, tiles))


def swap(x, axis, mask):
    size = lax.axis_size(axis)
    return lax.ppermute(x, axis, [(i, i ^ mask) for i in range(size)])


def near_rows(rows, again):
    step = lax.axis_size("blk") // 2
    here = [(0, rows), (step, swap(rows, "blk", step))]
    while step > 1:
        step //= 2
        direct = swap(again, "blk", step)
        here += [(step, direct)] + [(k | step, swap(relay(x, direct), "blk", step)) for k, x in here[1:]]
    return here


def bits(size, scale):
    return [scale << i for i in range(size.bit_length() - 1)]


def everywhere(mine, other):
    positions = lax.axis_size("blk")
    chips, places = bits(lax.axis_size("grp"), positions)[1:], bits(positions, 1)
    x = mine + swap(other, "grp", 1)
    while chips or places:
        a, b = chips[:1], places[:1]
        chips, places = chips[1:], places[1:]
        if a and b:
            x = (x + swap(x, AXES, a[0])) + (swap(x, AXES, b[0]) + swap(x, AXES, a[0] | b[0]))
        else:
            x = x + swap(x, AXES, (a + b)[0])
    return x, swap(x, "grp", 1)


def per_device(tiles_near, near_cols, tiles_far, far_groups, need_blocks, start_vectors):
    tile = tiles_near.shape[1]
    blocks = start_vectors.shape[0] // tile
    sources = lax.axis_size("blk")
    groups = lax.axis_size("grp")
    shape = (blocks, sources, tiles_near.shape[0] // (blocks * sources), tile)
    total_rows = start_vectors.shape[0] * sources * groups
    scalars = (near_cols, far_groups)
    wanted = swap(need_blocks, "grp", 1)
    split = 3 * sources // 4

    def begin(rows):
        below = prepare(rows, need_blocks.reshape(-1))
        far = [swap(below, "grp", k) for k in range(2, groups, 2)]
        near = near_rows(rows, rows)
        near[0] = (0, below)
        tiles = load(near[1][1], tiles_near, tiles_far)
        partial = near_product(shape, scalars, near[:split], tiles[0])
        tokens = [partial, *(x for _, x in near[split:])]
        far.append(swap(pack(tile, wanted, [below, *far], tokens), "grp", 1))
        partial = near_product(shape, scalars, near[split:], tiles[0], partial)
        return tiles, far, late(shape, scalars, need_blocks, partial, far, tiles[1])

    tiles, far, (product, rounded) = begin(start_vectors)
    past = gram(tile, product)
    own, *outs = blocks_for_others(tile, rounded, far, past)
    near = near_rows(rounded, rounded)
    far = [swap(x, "grp", 2 * i) for i, x in enumerate(outs, 1)]
    far.insert(0, swap(core_pack(own, far, near[1][1]), "grp", 1))
    partial = early(shape, groups, scalars, near[:split], far, *tiles)
    moved, *halves = last(shape, scalars, partial, near[split:], tiles[0], past)
    low, scale, both_low, next_scale, fine = factors(everywhere(*halves), total_rows)
    vectors = finish(dot3, moved, scale, both_low, next_scale)

    def plain(start, vectors, low, scale):
        _, _, (product, _) = begin(start)
        current = scaled(product, scale, low, dot6).astype(BF16)
        _, _, (product, _) = begin(current)
        unit = jnp.eye(product.shape[1], dtype=F32) * start.shape[0]
        halves = everywhere(*halves_of(unit, gram(tile, product)))
        _, scale, both_low, next_scale, _ = factors(halves, total_rows)
        return finish(dot6, product, scale, both_low, next_scale)

    branches = [plain, lambda start, vectors, low, scale: vectors]
    return lax.switch(fine[0], branches, start_vectors, vectors, low, scale)


def solution(mesh):
    in_specs = (
        P(AXES, None, None),
        P(AXES, None),
        P(AXES, None, None),
        P(AXES, None),
        P(AXES, None),
        P(AXES, None),
    )
    return jax.shard_map(
        per_device, mesh=mesh, in_specs=in_specs, out_specs=P(AXES, None), check_vma=False
    )
```
